512 devices in a mesh: row: 16 (over y, x_lo, core), col: 32 (over x_hi, z).
Axes of the slice: x: 4 (x_hi: 2, x_lo: 2; x = x_hi * 2 + x_lo), y: 4, z: 16, core: 2. Of those that a mesh axis runs over, the one named last changes fastest.
Arguments:
- pair: bfloat16 [768, 768, 128], P('row', 'col'), may hold values from -6 to 6
- pair_mask: int32 [768, 768], P('row', 'col'), may hold values from 0 to 1, as said below
- weights: bfloat16 [6, 128, 128], replicated, may hold values from -0.5 to 0.5
- cotangent: bfloat16 [768, 768, 128], P('row', 'col'), may hold values from -6 to 6
Outputs:
- update: bfloat16 [768, 768, 128], P('row', 'col')
- grad_pair: float32 [768, 768, 128], P('row', 'col')
- grad_weights: float32 [6, 128, 128], replicated
The draws below stay inside these ranges and needn't reach their ends.
Inputs may be any that keep to these rules, and one draw needn't show every extreme that they name: pair_mask[i, j] = m_i m_j with a residue mask m of 0 and 1: m_i is 0 for every residue at or past a padding length L, 576 <= L < 768, and for some residues before it.
All inputs are finite; a program needn't handle non-finite values.
Results may differ from the reference program's by a relative error of at most 0.012.
Values may be sent and summed in bfloat16 or wider, within the bound.
A program may use at most 64 MiB of HBM per device.

```python
import jax
import jax.numpy as jnp
from jax import lax

C = 128
N = 768


def draw_pair_mask(key, part):
    key = jax.random.fold_in(key, 11)
    length_key = jax.random.fold_in(key, 1)
    gap_key = jax.random.fold_in(key, 2)
    length = jax.random.randint(length_key, (), N - N // 4, N)
    positions = jnp.arange(N)
    resolved = jax.random.randint(gap_key, (N,), 0, 16) != 0
    valid = ((positions < length) & resolved).astype(jnp.int32)
    return valid[:, None] * valid[None, :]


def level_of(key, shape, pieces, least, high):
    level, own = 1.0, jax.random.fold_in(key, 6)
    for axis_at, parts in pieces:
        steps = jnp.exp(jax.random.uniform(jax.random.fold_in(own, axis_at), (parts,), jnp.float32, least / len(pieces), high / len(pieces)))
        level = level * jnp.repeat(steps, shape[axis_at] // parts).reshape([-1 if axis == axis_at else 1 for axis in range(len(shape))])
    return level


def noise(key, shape, spread, limit, split=(), dtype=jnp.bfloat16):
    level = level_of(key, shape, split, -0.22, 0.18) if split else 1.0
    result = jax.random.normal(key, shape, jnp.float32) * spread * level
    return jnp.minimum(jnp.maximum(result, -limit), limit).astype(dtype)


def setup_inputs(seed: int = 0) -> dict:
    keys = jax.random.split(jax.random.key(seed), 5)
    pair = noise(keys[0], (N, N, C), 1.0, 6.0, ((0, 16), (1, 32)))
    pair_mask = draw_pair_mask(jax.random.fold_in(keys[4], 71), 0)
    weights = noise(keys[2], (6, C, C), C ** -0.5, 0.5)
    cotangent = noise(keys[3], (N, N, C), 1.0, 6.0, ((0, 16), (1, 32)))
    return {"pair": pair, "pair_mask": pair_mask, "weights": weights, "cotangent": cotangent}


def normalize(values):
    average = lax.optimization_barrier(jnp.mean(values, axis=-1, keepdims=True))
    centred = values - average
    variance = lax.optimization_barrier(jnp.mean(centred * centred, axis=-1, keepdims=True))
    inverse = lax.rsqrt(variance + 1e-05)
    return (centred * inverse, inverse)

def norm_backward(upstream, normed, inverse):
    first = lax.optimization_barrier(jnp.mean(upstream, axis=-1, keepdims=True))
    second = lax.optimization_barrier(jnp.mean(upstream * normed, axis=-1, keepdims=True))
    return inverse * (upstream - first - normed * second)

def reference(pair, pair_mask, weights, cotangent):
    residues = pair.shape[0]
    channels = pair.shape[2]
    normed_in, inv_in = normalize(pair.astype(jnp.float32))
    flat_in = normed_in.astype(jnp.bfloat16).reshape(residues * residues, channels)
    projected = [jnp.dot(flat_in, weights[number], preferred_element_type=jnp.float32).reshape(residues, residues, channels) for number in range(5)]
    mask_float = pair_mask.astype(jnp.float32)[..., None]
    left_sig = jax.nn.sigmoid(projected[1])
    right_sig = jax.nn.sigmoid(projected[3])
    left_act = (mask_float * left_sig * projected[0]).astype(jnp.bfloat16)
    right_act = (mask_float * right_sig * projected[2]).astype(jnp.bfloat16)
    triangle = jnp.einsum('ikc,jkc->ijc', left_act.astype(jnp.float32), right_act.astype(jnp.float32)).astype(jnp.bfloat16)
    normed_out, inv_out = normalize(triangle.astype(jnp.float32))
    flat_out = normed_out.astype(jnp.bfloat16).reshape(residues * residues, channels)
    linear = jnp.dot(flat_out, weights[5], preferred_element_type=jnp.float32).reshape(residues, residues, channels)
    gate_sig = jax.nn.sigmoid(projected[4])
    update = (gate_sig * linear).astype(jnp.bfloat16)
    upstream = cotangent.astype(jnp.float32)
    grad_linear = (upstream * gate_sig).astype(jnp.bfloat16)
    grad_logit = (upstream * linear * gate_sig * (1.0 - gate_sig)).astype(jnp.bfloat16)
    grad_xout = jnp.dot(grad_linear.reshape(-1, channels), weights[5].T, preferred_element_type=jnp.float32).reshape(residues, residues, channels)
    grad_tri = norm_backward(grad_xout, normed_out, inv_out).astype(jnp.bfloat16)
    grad_left = jnp.einsum('ijc,jkc->ikc', grad_tri.astype(jnp.float32), right_act.astype(jnp.float32)).astype(jnp.bfloat16)
    grad_right = jnp.einsum('ijc,ikc->jkc', grad_tri.astype(jnp.float32), left_act.astype(jnp.float32)).astype(jnp.bfloat16)
    left_float = grad_left.astype(jnp.float32) * mask_float
    right_float = grad_right.astype(jnp.float32) * mask_float
    grads = [(left_float * left_sig).astype(jnp.bfloat16), (left_float * projected[0] * left_sig * (1.0 - left_sig)).astype(jnp.bfloat16), (right_float * right_sig).astype(jnp.bfloat16), (right_float * projected[2] * right_sig * (1.0 - right_sig)).astype(jnp.bfloat16), grad_logit]
    grad_xin = jnp.zeros((residues * residues, channels), jnp.float32)
    for number in range(5):
        grad_xin = grad_xin + jnp.dot(grads[number].reshape(-1, channels), weights[number].T, preferred_element_type=jnp.float32)
    grad_pair = norm_backward(grad_xin.reshape(residues, residues, channels), normed_in, inv_in)
    weight_list = [jnp.dot(flat_in.T, grads[number].reshape(-1, channels), preferred_element_type=jnp.float32) for number in range(5)]
    weight_list.append(jnp.dot(flat_out.T, grad_linear.reshape(-1, channels), preferred_element_type=jnp.float32))
    grad_weights = jnp.stack(weight_list) / jnp.float32(residues)
    return (update, grad_pair, grad_weights)
```

```python
import jax
import jax.numpy as jnp
from jax import lax
from jax.sharding import PartitionSpec as P


def normalize(values):
    average = jnp.mean(values, axis=-1, keepdims=True)
    centred = values - average
    variance = jnp.mean(centred * centred, axis=-1, keepdims=True)
    inverse = lax.rsqrt(variance + 1e-05)
    return (centred * inverse, inverse)


def norm_backward(upstream, normed, inverse):
    first = jnp.mean(upstream, axis=-1, keepdims=True)
    second = jnp.mean(upstream * normed, axis=-1, keepdims=True)
    return inverse * (upstream - first - normed * second)


def on_device(pair, pair_mask, weights, cotangent):
    row_count, col_count, channels = pair.shape
    residues = row_count * lax.axis_size("row")
    pixels = row_count * col_count
    normed_in, inv_in = normalize(pair.astype(jnp.float32))
    flat_in = normed_in.astype(jnp.bfloat16).reshape(pixels, channels)
    weight_in = jnp.concatenate([weights[number] for number in range(5)], axis=1)
    projected_all = jnp.dot(flat_in, weight_in, preferred_element_type=jnp.float32).reshape(
        row_count, col_count, 5 * channels
    )
    projected = [
        projected_all[..., number * channels : (number + 1) * channels] for number in range(5)
    ]
    mask_float = pair_mask.astype(jnp.float32)[..., None]
    left_sig = jax.nn.sigmoid(projected[1])
    right_sig = jax.nn.sigmoid(projected[3])
    left_act = (mask_float * left_sig * projected[0]).astype(jnp.bfloat16)
    right_act = (mask_float * right_sig * projected[2]).astype(jnp.bfloat16)
    left_chan, right_chan = (
        lax.all_to_all(left_act.transpose(2, 0, 1), "col", split_axis=0, concat_axis=2, tiled=True),
        lax.all_to_all(
            right_act.transpose(2, 0, 1), "col", split_axis=0, concat_axis=2, tiled=True
        ),
    )
    right_full = lax.all_gather(right_chan, "row", axis=1, tiled=True)
    tri_chan = jnp.einsum(
        "cik,cjk->cij", left_chan, right_full, preferred_element_type=jnp.float32
    ).astype(jnp.bfloat16)
    tri_tile = lax.all_to_all(tri_chan, "col", split_axis=2, concat_axis=0, tiled=True)
    normed_out, inv_out = normalize(tri_tile.transpose(1, 2, 0).astype(jnp.float32))
    flat_out = normed_out.astype(jnp.bfloat16).reshape(pixels, channels)
    linear = jnp.dot(flat_out, weights[5], preferred_element_type=jnp.float32).reshape(
        row_count, col_count, channels
    )
    gate_sig = jax.nn.sigmoid(projected[4])
    update = (gate_sig * linear).astype(jnp.bfloat16)
    upstream = cotangent.astype(jnp.float32)
    grad_linear = (upstream * gate_sig).astype(jnp.bfloat16)
    grad_logit = (upstream * linear * gate_sig * (1.0 - gate_sig)).astype(jnp.bfloat16)
    linear_flat = grad_linear.reshape(pixels, channels)
    grad_xout = jnp.dot(linear_flat, weights[5].T, preferred_element_type=jnp.float32).reshape(
        row_count, col_count, channels
    )
    grad_tri = norm_backward(grad_xout, normed_out, inv_out).astype(jnp.bfloat16)
    grad_chan = lax.all_to_all(
        grad_tri.transpose(2, 0, 1), "col", split_axis=0, concat_axis=2, tiled=True
    )
    left_grad_chan = jnp.einsum(
        "cij,cjk->cik", grad_chan, right_full, preferred_element_type=jnp.float32
    ).astype(jnp.bfloat16)
    own_start = lax.axis_index("row") * row_count
    grad_piece = lax.all_gather(grad_chan, "row", axis=1, tiled=True)
    left_piece = lax.all_gather(left_chan, "row", axis=1, tiled=True)
    selected = lax.dynamic_slice_in_dim(grad_piece, own_start, row_count, 2)
    right_grad_chan = jnp.einsum(
        "cij,cik->cjk", selected, left_piece, preferred_element_type=jnp.float32
    ).astype(jnp.bfloat16)
    left_back, right_back = (
        lax.all_to_all(left_grad_chan, "col", split_axis=2, concat_axis=0, tiled=True),
        lax.all_to_all(right_grad_chan, "col", split_axis=2, concat_axis=0, tiled=True),
    )
    left_float = left_back.transpose(1, 2, 0).astype(jnp.float32) * mask_float
    right_float = right_back.transpose(1, 2, 0).astype(jnp.float32) * mask_float
    grads = [
        (left_float * left_sig).astype(jnp.bfloat16),
        (left_float * projected[0] * left_sig * (1.0 - left_sig)).astype(jnp.bfloat16),
        (right_float * right_sig).astype(jnp.bfloat16),
        (right_float * projected[2] * right_sig * (1.0 - right_sig)).astype(jnp.bfloat16),
        grad_logit,
    ]
    grad_stack = jnp.concatenate(grads, axis=-1).reshape(pixels, 5 * channels)
    grad_xin = jnp.dot(grad_stack, weight_in.T, preferred_element_type=jnp.float32).reshape(
        row_count, col_count, channels
    )
    grad_pair = norm_backward(grad_xin, normed_in, inv_in)
    input_terms = jnp.einsum("pc,pd->cd", flat_in, grad_stack, preferred_element_type=jnp.float32)
    output_terms = jnp.einsum(
        "pc,pd->cd", flat_out, linear_flat, preferred_element_type=jnp.float32
    )
    terms = [input_terms[:, number * channels : (number + 1) * channels] for number in range(5)]
    terms = jnp.stack(terms + [output_terms])
    rows, cols = lax.axis_size("row"), lax.axis_size("col")
    share = lax.all_to_all(terms.reshape(rows, -1), "row", 0, 0, tiled=True).sum(axis=0)
    share = lax.all_to_all(share.reshape(cols, -1), "col", 0, 0, tiled=True).sum(axis=0)
    share = lax.all_to_all(
        jnp.broadcast_to(share, (cols,) + share.shape), "col", 0, 0, tiled=True
    ).reshape(-1)
    share = lax.all_to_all(
        jnp.broadcast_to(share, (rows,) + share.shape), "row", 0, 0, tiled=True
    )
    grad_weights = share.reshape(terms.shape) / jnp.float32(residues)
    return (update, grad_pair, grad_weights)


def solution(mesh):
    placed = (P("row", "col", None), P("row", "col"), P(), P("row", "col", None))
    return jax.shard_map(
        on_device,
        mesh=mesh,
        in_specs=placed,
        out_specs=(P("row", "col", None), P("row", "col", None), P()),
        check_vma=False,
    )
```

```python
import functools

import jax
import jax.numpy as jnp
import numpy as np
from jax import lax
from jax.experimental import pallas as pl
from jax.experimental.pallas import tpu as pltpu
from jax.sharding import PartitionSpec as P


F32 = jnp.float32
BF16 = jnp.bfloat16
C = 128
BLOCKS = 9
Y, S, Q, R = 4, 4, 32, 16
ROWS = 192
WIDE = 1024
PAIRED, SINGLE = 80, 48
MESH = pl.DeviceIdType.MESH


def nt(a, b):
    return lax.dot_general(a, b, (((1,), (1,)), ((), ())), preferred_element_type=F32)


def nn(a, b):
    return lax.dot_general(a, b, (((1,), (0,)), ((), ())), preferred_element_type=F32)


def tn(a, b):
    return lax.dot_general(a, b, (((0,), (0,)), ((), ())), preferred_element_type=F32)


def normalize(values):
    average = jnp.mean(values, axis=0, keepdims=True)
    centred = values - average
    variance = jnp.mean(centred * centred, axis=0, keepdims=True)
    inverse = lax.rsqrt(variance + 1e-05)
    return centred * inverse, inverse


def norm_backward(upstream, normed, inverse):
    first = jnp.mean(upstream, axis=0, keepdims=True)
    second = jnp.mean(upstream * normed, axis=0, keepdims=True)
    return inverse * (upstream - first - normed * second)


def column_order():
    low, block, tile = np.meshgrid(np.arange(8), np.arange(3), np.arange(Q), indexing="ij")
    residue = (tile * 24 + block * 8 + low).reshape(-1)
    place = (low * 128 + block * 32 + tile).reshape(-1)
    y, s, inner = residue // 192, residue // 48 % 4, residue % 48
    order = np.zeros((S, WIDE, 256), np.float32)
    order[s, place, y * 48 + inner] = 1
    return order.astype(jnp.bfloat16)


def loop(count, body):
    def step(i, carry):
        body(i)
        return carry

    lax.fori_loop(0, count, step, 0)


def kernel(
    pair_ref,
    cot_ref,
    mask_ref,
    win_ref,
    wback_ref,
    wout_ref,
    woutb_ref,
    order_ref,
    upd_ref,
    gpair_ref,
    gw_ref,
    proj,
    xn,
    xb,
    inv,
    logit,
    flat,
    ys_a,
    yr_a,
    zs_a,
    zr_a,
    ys_t,
    yr_t,
    zs_t,
    zr_t,
    ys_g,
    yr_g,
    zs_g,
    zr_g,
    ys_b,
    yr_b,
    zs_b,
    zr_b,
    left,
    right,
    gmat,
    acc,
    gs,
    gr,
    gw5,
    gwin,
    wfull,
    ws1,
    wr1,
    ws2,
    wr2,
    ws3,
    wr3,
    y_send,
    y_recv,
    z_send,
    z_recv,
    s_send,
    s_recv,
    w1_send,
    w1_recv,
    w2_send,
    w2_recv,
    w3_send,
    w3_recv,
):
    r = lax.axis_index("row")
    q = lax.axis_index("col")
    y = r // 4
    s = r % 4
    barrier = pltpu.get_barrier_semaphore()

    def signal_col(d):
        pl.semaphore_signal(
            barrier, inc=1, device_id={"row": r, "col": (q + 1 + d) % Q}, device_id_type=MESH
        )

    def signal_row(d):
        pl.semaphore_signal(
            barrier, inc=1, device_id={"row": (r + 1 + d) % R, "col": q}, device_id_type=MESH
        )

    loop(Q - 1, signal_col)
    loop(R - 1, signal_row)

    def partner(step):
        u = Q - 1 - step
        t = u // 2
        hop = ((t + 1) // 2) * (2 * (t % 2) - 1)
        z = (q % 16 + hop + 16) % 16
        return ((q // 16 + u) % 2) * 16 + z

    def y_copy(phase, src, dst, d):
        to = (y + 1 + d) % Y
        return pltpu.make_async_remote_copy(
            src_ref=src.at[to],
            dst_ref=dst.at[y],
            send_sem=y_send.at[phase, to],
            recv_sem=y_recv.at[phase, y],
            device_id={"row": to * 4 + s, "col": q},
            device_id_type=MESH,
        )

    def y_wait(phase, src, dst, d):
        frm = (y + 1 + d) % Y
        pltpu.make_async_remote_copy(
            src_ref=src.at[frm],
            dst_ref=dst.at[frm],
            send_sem=y_send.at[phase, frm],
            recv_sem=y_recv.at[phase, frm],
            device_id={"row": frm * 4 + s, "col": q},
            device_id_type=MESH,
        ).wait_recv()

    def y_exchange(phase, src, dst):
        loop(Y - 1, lambda d: y_copy(phase, src, dst, d).start())
        dst[y] = src[y]
        loop(Y - 1, lambda d: y_wait(phase, src, dst, d))

    def z_copy(phase, src, dst, to):
        return pltpu.make_async_remote_copy(
            src_ref=src.at[to],
            dst_ref=dst.at[q],
            send_sem=z_send.at[phase, to],
            recv_sem=z_recv.at[phase, q],
            device_id={"row": r, "col": to},
            device_id_type=MESH,
        )

    def z_exchange(phase, src, dst, rows, make):
        def send(step):
            to = partner(step)
            src[to] = make(to)
            z_copy(phase, src, dst, to).start()

        def receive(step):
            frm = partner(Q - 2 - step)
            pltpu.make_async_remote_copy(
                src_ref=src.at[frm],
                dst_ref=dst.at[frm],
                send_sem=z_send.at[phase, frm],
                recv_sem=z_recv.at[phase, frm],
                device_id={"row": r, "col": frm},
                device_id_type=MESH,
            ).wait_recv()
            flat[pl.ds(pl.multiple_of(frm * rows, 16), rows), :] = dst[frm].astype(F32)

        loop(Q - 1, send)
        dst[q] = make(q)
        flat[pl.ds(pl.multiple_of(q * rows, 16), rows), :] = dst[q].astype(F32)
        loop(Q - 1, receive)

    def spread(arrays, recv):
        def body(step):
            yy, block = step // (arrays * BLOCKS), step % (arrays * BLOCKS)
            row = (block // BLOCKS) * 36 + yy * BLOCKS + block % BLOCKS
            flat[pl.ds(pl.multiple_of(row * 32, 32), 32), :] = recv[yy, block].astype(F32)

        loop(Y * arrays * BLOCKS, body)

    def pick(rows):
        return lambda to: flat[pl.ds(to, rows, stride=32), :].astype(BF16)

    def stored(rows):
        return lambda to: flat[pl.ds(pl.multiple_of(to * rows, 16), rows), :].astype(BF16)

    def gather_up(arrays, rows, send):
        def body(step):
            yy, block = step // (arrays * BLOCKS), step % (arrays * BLOCKS)
            row = (block // BLOCKS) * 36 + yy * BLOCKS + block % BLOCKS
            send[yy, block] = flat[pl.ds(row, Q, stride=rows), :].astype(BF16)

        loop(Y * arrays * BLOCKS, body)

    def to_matrix(first, rows, write):
        def body(step):
            parts = [flat[pl.ds(first + 3 * step + b, Q, stride=rows), :] for b in range(3)]
            turned = jnp.concatenate(parts + [jnp.zeros((Q, C), F32)], axis=0).T.astype(BF16)
            for low in range(8):
                write(
                    pl.ds(pl.multiple_of(step * 16, 16), 16),
                    slice(low * 128, low * 128 + 128),
                    turned[low * 16 : low * 16 + 16],
                )

        loop(12, body)

    def from_matrix(first, rows):
        def body(step):
            at = pl.ds(pl.multiple_of(step * 16, 16), 16)
            parts = [acc[at, low * 128 : low * 128 + 128] for low in range(8)]
            turned = jnp.concatenate(parts, axis=0).T
            for b in range(3):
                flat[pl.ds(first + 3 * step + b, Q, stride=rows), :] = turned[b * 32 : b * 32 + 32]

        loop(12, body)

    def mate(d):
        return ((s // 2 + (d + 1) // 2) % 2) * 2 + (s % 2 + (d + 1) % 2) % 2

    def s_copy(phase, src, dst, d):
        to = mate(d)
        return pltpu.make_async_remote_copy(
            src_ref=src(to),
            dst_ref=dst.at[s],
            send_sem=s_send.at[phase, to],
            recv_sem=s_recv.at[phase, s],
            device_id={"row": y * 4 + to, "col": q},
            device_id_type=MESH,
        )

    def s_wait(phase, dst, frm):
        pltpu.make_async_remote_copy(
            src_ref=dst.at[frm],
            dst_ref=dst.at[frm],
            send_sem=s_send.at[phase, frm],
            recv_sem=s_recv.at[phase, frm],
            device_id={"row": y * 4 + frm, "col": q},
            device_id_type=MESH,
        ).wait_recv()

    def s_send_wait(phase, src, dst):
        loop(3, lambda d: s_copy(phase, src, dst, d).wait_send())

    def project(block):
        normed, inverse = normalize(pair_ref[block].astype(F32).T)
        rounded = normed.astype(BF16)
        xn[block] = normed
        xb[block] = rounded
        inv[block] = inverse
        p = nn(win_ref[...], rounded)
        proj[block] = p
        mask = mask_ref[block]
        values = (
            (mask * jax.nn.sigmoid(p[C : 2 * C]) * p[:C]).astype(BF16),
            (mask * jax.nn.sigmoid(p[3 * C : 4 * C]) * p[2 * C : 3 * C]).astype(BF16),
        )
        for array in range(2):
            for yy in range(Y):
                ys_a[yy, array * BLOCKS + block] = values[array][yy * 32 : yy * 32 + 32]

    loop(BLOCKS, project)
    pl.semaphore_wait(barrier, Q + R - 2)

    flat[72 * 32 :, :] = jnp.zeros((8 * 32, C), F32)
    y_exchange(0, ys_a, yr_a)
    spread(2, yr_a)
    z_exchange(0, zs_a, zr_a, PAIRED, pick(PAIRED))

    def write_to(ref, *index):
        def write(rows, columns, value):
            ref[(*index, rows, columns)] = value

        return write

    to_matrix(36, PAIRED, write_to(right, s))
    loop(3, lambda d: s_copy(0, lambda to: right.at[s], right, d).start())
    to_matrix(0, PAIRED, write_to(left, s))
    loop(3, lambda d: s_copy(1, lambda to: left.at[s], left, d).start())

    acc[...] = jnp.zeros_like(acc)

    def triangle(part):
        tri = nt(left[s], right[part]).astype(BF16)
        acc[...] += nt(tri, order_ref[part][:, :ROWS])

    triangle(s)

    def triangle_step(d):
        s_wait(0, right, mate(d))
        triangle(mate(d))

    loop(3, triangle_step)
    from_matrix(0, SINGLE)
    z_exchange(1, zs_t, zr_t, SINGLE, stored(SINGLE))
    gather_up(1, SINGLE, ys_t)
    y_exchange(1, ys_t, yr_t)

    gw5[...] = jnp.zeros_like(gw5)

    def tile(block):
        tri = jnp.concatenate([yr_t[yy, block] for yy in range(Y)], axis=0).astype(F32)
        normed, inverse = normalize(tri)
        rounded = normed.astype(BF16)
        linear = nn(wout_ref[...], rounded)
        gate = jax.nn.sigmoid(proj[block, 4 * C : 5 * C])
        upd_ref[block] = (gate * linear).T.astype(BF16)
        upstream = cot_ref[block].astype(F32).T
        grad_linear = (upstream * gate).astype(BF16)
        logit[block] = (upstream * linear * gate * (1.0 - gate)).astype(BF16)
        gw5[...] += nt(rounded, grad_linear)
        grad_tri = norm_backward(nn(woutb_ref[...], grad_linear), normed, inverse).astype(BF16)
        for yy in range(Y):
            ys_g[yy, block] = grad_tri[yy * 32 : yy * 32 + 32]

    loop(BLOCKS, tile)
    y_exchange(2, ys_g, yr_g)
    spread(1, yr_g)
    z_exchange(2, zs_g, zr_g, SINGLE, pick(SINGLE))
    to_matrix(0, SINGLE, write_to(gmat))

    def columns_of(part):
        gs[part] = nn(gmat[...], order_ref[part]).astype(BF16)

    loop(S, columns_of)
    loop(3, lambda d: s_copy(2, lambda to: gs.at[to], gr, d).start())
    gr[s] = gs[s]
    acc[...] = jnp.zeros_like(acc)

    def grad_left(part):
        acc[...] += nn(gs[part][:, :ROWS], right[part])

    loop(S, grad_left)
    from_matrix(0, PAIRED)
    acc[...] = jnp.zeros_like(acc)

    def grad_right(part):
        acc[...] += tn(gr[part][:, :ROWS], left[part])

    grad_right(s)

    def grad_right_step(d):
        s_wait(1, left, mate(d))
        s_wait(2, gr, mate(d))
        grad_right(mate(d))

    loop(3, grad_right_step)
    from_matrix(36, PAIRED)
    z_exchange(3, zs_b, zr_b, PAIRED, stored(PAIRED))
    gather_up(2, PAIRED, ys_b)
    y_exchange(3, ys_b, yr_b)

    gwin[...] = jnp.zeros_like(gwin)

    def finish(block):
        mask = mask_ref[block]
        grads = []
        for array in range(2):
            parts = [yr_b[yy, array * BLOCKS + block] for yy in range(Y)]
            upstream = jnp.concatenate(parts, axis=0).astype(F32) * mask
            value = proj[block, 2 * array * C : (2 * array + 1) * C]
            gate = jax.nn.sigmoid(proj[block, (2 * array + 1) * C : (2 * array + 2) * C])
            grads.append((upstream * gate).astype(BF16))
            grads.append((upstream * value * gate * (1.0 - gate)).astype(BF16))
        stack = jnp.concatenate(grads + [logit[block]], axis=0)
        grad = norm_backward(nn(wback_ref[...], stack), xn[block], inv[block])
        gpair_ref[block] = grad.T
        gwin[...] += nt(xb[block], stack)

    loop(BLOCKS, finish)

    for m in range(5):
        wfull[m * C : (m + 1) * C] = gwin[:, m * C : (m + 1) * C]
    wfull[5 * C :] = gw5[...]
    for part in range(R):
        ws1[part] = wfull[part * 48 : part * 48 + 48].astype(BF16)

    def other_row(d):
        return (r + 1 + d) % R

    def other_col(d):
        return (q + 1 + d) % Q

    def w1_copy(to, at):
        return pltpu.make_async_remote_copy(
            src_ref=ws1.at[to],
            dst_ref=wr1.at[at],
            send_sem=w1_send.at[to],
            recv_sem=w1_recv.at[at],
            device_id={"row": to, "col": q},
            device_id_type=MESH,
        )

    def w2_copy(to, at):
        return pltpu.make_async_remote_copy(
            src_ref=ws2,
            dst_ref=wr2.at[at],
            send_sem=w2_send.at[to],
            recv_sem=w2_recv.at[at],
            device_id={"row": r, "col": to},
            device_id_type=MESH,
        )

    def w3_copy(to, at):
        return pltpu.make_async_remote_copy(
            src_ref=ws3,
            dst_ref=wr3.at[at],
            send_sem=w3_send.at[to],
            recv_sem=w3_recv.at[at],
            device_id={"row": to, "col": q},
            device_id_type=MESH,
        )

    loop(R - 1, lambda d: w1_copy(other_row(d), r).start())
    wr1[r] = ws1[r]
    loop(R - 1, lambda d: w1_copy(other_row(d), other_row(d)).wait_recv())
    ws2[...] = sum(wr1[part].astype(F32) for part in range(R)).astype(BF16)
    loop(Q - 1, lambda d: w2_copy(partner(d), q).start())
    wr2[q] = ws2[...]
    loop(Q - 1, lambda d: w2_copy(other_col(d), other_col(d)).wait_recv())
    ws3[...] = sum(wr2[part].astype(F32) for part in range(Q)) * (1.0 / (R * 48))
    loop(R - 1, lambda d: w3_copy(other_row(d), r).start())
    wr3[r] = ws3[...]
    loop(R - 1, lambda d: w3_copy(other_row(d), other_row(d)).wait_recv())
    gw_ref[...] = wr3[...]

    for phase, (src, dst) in enumerate(((ys_a, yr_a), (ys_t, yr_t), (ys_g, yr_g), (ys_b, yr_b))):
        loop(Y - 1, lambda d, p=phase, a=src, b=dst: y_copy(p, a, b, d).wait_send())
    for phase, (src, dst) in enumerate(((zs_a, zr_a), (zs_t, zr_t), (zs_g, zr_g), (zs_b, zr_b))):
        loop(Q - 1, lambda d, p=phase, a=src, b=dst: z_copy(p, a, b, other_col(d)).wait_send())
    s_send_wait(0, lambda to: right.at[s], right)
    s_send_wait(1, lambda to: left.at[s], left)
    s_send_wait(2, lambda to: gs.at[to], gr)
    loop(R - 1, lambda d: w1_copy(other_row(d), r).wait_send())
    loop(Q - 1, lambda d: w2_copy(other_col(d), q).wait_send())
    loop(R - 1, lambda d: w3_copy(other_row(d), r).wait_send())


def on_device(pair, pair_mask, weights, cotangent):
    def blocks(values, tail):
        values = values.reshape((3, 16, 3, 8) + tail)
        return values.transpose((0, 2, 3, 1) + tuple(range(4, 4 + len(tail))))

    def tile(values):
        values = values.reshape(3, 3, 8, 16, C).transpose(0, 3, 1, 2, 4)
        return values.reshape(48, 24, C)

    pair_in = blocks(pair, (C,)).reshape(BLOCKS, C, C)
    cot_in = blocks(cotangent, (C,)).reshape(BLOCKS, C, C)
    mask_in = blocks(pair_mask.astype(F32), ()).reshape(BLOCKS, 1, C)
    win = weights[:5].transpose(0, 2, 1).reshape(5 * C, C)
    wback = weights[:5].transpose(1, 0, 2).reshape(C, 5 * C)
    vmem = pl.BlockSpec(memory_space=pltpu.VMEM)

    def y_pair(arrays):
        return [pltpu.VMEM((Y, arrays * BLOCKS, 32, C), BF16)] * 2

    def z_pair(rows):
        return [pltpu.VMEM((Q, rows, C), BF16)] * 2

    def sems(*shape):
        return [pltpu.SemaphoreType.DMA(shape)] * 2

    update, grad_pair, grad_weights = pl.pallas_call(
        kernel,
        out_shape=(
            jax.ShapeDtypeStruct((BLOCKS, C, C), BF16),
            jax.ShapeDtypeStruct((BLOCKS, C, C), F32),
            jax.ShapeDtypeStruct((R, 48, C), F32),
        ),
        in_specs=[vmem] * 8,
        out_specs=(vmem, vmem, vmem),
        scratch_shapes=[
            pltpu.VMEM((BLOCKS, 5 * C, C), F32),
            pltpu.VMEM((BLOCKS, C, C), F32),
            pltpu.VMEM((BLOCKS, C, C), BF16),
            pltpu.VMEM((BLOCKS, 1, C), F32),
            pltpu.VMEM((BLOCKS, C, C), BF16),
            pltpu.VMEM((Q * PAIRED, C), F32),
            *y_pair(2),
            *z_pair(PAIRED),
            *y_pair(1),
            *z_pair(SINGLE),
            *y_pair(1),
            *z_pair(SINGLE),
            *y_pair(2),
            *z_pair(PAIRED),
            pltpu.VMEM((S, ROWS, WIDE), BF16),
            pltpu.VMEM((S, ROWS, WIDE), BF16),
            pltpu.VMEM((ROWS, WIDE), BF16),
            pltpu.VMEM((ROWS, WIDE), F32),
            pltpu.VMEM((S, ROWS, 256), BF16),
            pltpu.VMEM((S, ROWS, 256), BF16),
            pltpu.VMEM((C, C), F32),
            pltpu.VMEM((C, 5 * C), F32),
            pltpu.VMEM((6 * C, C), F32),
            pltpu.VMEM((R, 48, C), BF16),
            pltpu.VMEM((R, 48, C), BF16),
            pltpu.VMEM((48, C), BF16),
            pltpu.VMEM((Q, 48, C), BF16),
            pltpu.VMEM((48, C), F32),
            pltpu.VMEM((R, 48, C), F32),
            *sems(4, Y),
            *sems(4, Q),
            *sems(3, S),
            *sems(R),
            *sems(Q),
            *sems(R),
        ],
        compiler_params=pltpu.CompilerParams(
            collective_id=0, has_side_effects=True, vmem_limit_bytes=56 * 1024 * 1024
        ),
    )(pair_in, cot_in, mask_in, win, wback, weights[5].T, weights[5], jnp.asarray(column_order()))
    return tile(update), tile(grad_pair), grad_weights.reshape(6, C, C)


def solution(mesh):
    placed = (P("row", "col", None), P("row", "col"), P(), P("row", "col", None))
    return jax.shard_map(
        on_device,
        mesh=mesh,
        in_specs=placed,
        out_specs=(P("row", "col", None), P("row", "col", None), P()),
        check_vma=False,
    )
```

```python
import jax
import jax.numpy as jnp
import numpy as np
from jax import lax
from jax.experimental import pallas as pl
from jax.experimental.pallas import tpu as pltpu
from jax.sharding import PartitionSpec as P


F32 = jnp.float32
BF16 = jnp.bfloat16
C = 128
BLOCKS = 9
Y, S, Z, G = 4, 4, 16, 8
ROWS = 192
WIDE = 1024
TILE_ROWS = 384
MESH = pl.DeviceIdType.MESH
RIGHT, LEFT, TRI0, TRI1, GRAD0, GRAD1, BACK_L, BACK_R = range(8)
PHASES = ((9, 80), (9, 80), (3, 32), (6, 48), (3, 32), (6, 48), (9, 80), (9, 80))
PARTS = ((0, 1), (1, 2))


def nt(a, b):
    return lax.dot_general(a, b, (((1,), (1,)), ((), ())), preferred_element_type=F32)


def nn(a, b):
    return lax.dot_general(a, b, (((1,), (0,)), ((), ())), preferred_element_type=F32)


def normalize(values):
    average = jnp.mean(values, axis=0, keepdims=True)
    centred = values - average
    variance = jnp.mean(centred * centred, axis=0, keepdims=True)
    inverse = lax.rsqrt(variance + 1e-05)
    return centred * inverse, inverse


def norm_backward(upstream, normed, inverse):
    first = jnp.mean(upstream, axis=0, keepdims=True)
    second = jnp.mean(upstream * normed, axis=0, keepdims=True)
    return inverse * (upstream - first - normed * second)


def column_order():
    low, block, tile = np.meshgrid(np.arange(8), np.arange(3), np.arange(32), indexing="ij")
    residue = (tile * 24 + block * 8 + low).reshape(-1)
    place = (low * 128 + block * 32 + tile).reshape(-1)
    y, s, inner = residue // 192, residue // 48 % 4, residue % 48
    order = np.zeros((S, ROWS, WIDE), np.float32)
    order[s, y * 48 + inner, place] = 1
    return order.astype(jnp.bfloat16)


def loop(count, body):
    def step(i, carry):
        body(i)
        return carry

    lax.fori_loop(0, count, step, 0)


def at(start, size, unit=8):
    return pl.ds(pl.multiple_of(start * unit, unit), size)


def kernel(
    pair_hbm,
    cot_hbm,
    order_hbm,
    mask_ref,
    weights_ref,
    upd_hbm,
    gpair_hbm,
    gw_ref,
    pair_v,
    cot_v,
    order,
    upd_v,
    gpair_v,
    wt,
    wback,
    proj,
    xn,
    xb,
    inv,
    stack,
    flat,
    turned,
    left,
    right,
    gmat,
    tri,
    gs,
    gts,
    gtr,
    gwin,
    *rest,
):
    rest = list(rest)
    ys, yr, zs, zr = ([rest.pop(0) for _ in PHASES] for _ in range(4))
    sums = [[rest.pop(0) for _ in range(9)] for _ in range(2)]
    y_send, y_recv, z_send, z_recv, s_send, s_recv = (rest.pop(0) for _ in range(6))
    w_sems = [[rest.pop(0) for _ in range(10)] for _ in range(2)]
    local = rest.pop(0)

    r = lax.axis_index("row")
    q = lax.axis_index("col")
    y, s = r // 4, r % 4
    half, z = q // 16, q % 16
    g = y * 2 + half

    def group(other):
        return {"row": (other // 2) * 4 + s, "col": (other % 2) * 16 + z}

    def along(other):
        return {"row": r, "col": half * 16 + other}

    def mate(d):
        return ((s // 2 + (d + 1) // 2) % 2) * 2 + (s % 2 + (d + 1) % 2) % 2

    def shared(other):
        return {"row": y * 4 + other, "col": q}

    def next_g(d):
        return (g + 1 + d) % G

    def next_z(step):
        t = Z - 1 - step
        hop = ((t + 1) // 2) * (2 * (t % 2) - 1)
        return (z + hop + Z) % Z

    barrier = pltpu.get_barrier_semaphore()

    def greet(device):
        pl.semaphore_signal(barrier, inc=1, device_id=device, device_id_type=MESH)

    loop(Z - 1, lambda d: greet(along(next_z(d))))
    loop(G - 1, lambda d: greet(group(next_g(d))))
    loop(S - 1, lambda d: greet(shared(mate(d))))

    load_pair = pltpu.make_async_copy(pair_hbm, pair_v, local.at[0])
    load_cot = pltpu.make_async_copy(cot_hbm, cot_v, local.at[1])
    load_order = pltpu.make_async_copy(order_hbm, order, local.at[2])
    load_pair.start()
    load_cot.start()
    load_order.start()

    def y_copy(phase, to, slot):
        return pltpu.make_async_remote_copy(
            src_ref=ys[phase].at[to],
            dst_ref=yr[phase].at[slot],
            send_sem=y_send.at[phase, to],
            recv_sem=y_recv.at[phase, slot],
            device_id=group(to),
            device_id_type=MESH,
        )

    def y_start(phase):
        loop(G - 1, lambda d: y_copy(phase, next_g(d), g).start())
        yr[phase][g] = ys[phase][g]

    def y_wait(phase):
        loop(G - 1, lambda d: y_copy(phase, next_g(d), next_g(d)).wait_recv())

    def z_copy(phase, to, slot):
        return pltpu.make_async_remote_copy(
            src_ref=zs[phase].at[to],
            dst_ref=zr[phase].at[slot],
            send_sem=z_send.at[phase, to],
            recv_sem=z_recv.at[phase, slot],
            device_id=along(to),
            device_id_type=MESH,
        )

    def z_start(phase, make):
        def send(step):
            to = next_z(step)
            zs[phase][to] = make(to)
            z_copy(phase, to, z).start()

        loop(Z - 1, send)
        zr[phase][z] = make(z)

    def z_wait(phase):
        rows = PHASES[phase][1]

        def receive(step):
            frm = next_z(Z - 2 - step)
            z_copy(phase, frm, frm).wait_recv()
            flat[at(frm * (rows // 16), rows, 16), :] = zr[phase][frm].astype(F32)

        flat[at(z * (rows // 16), rows, 16), :] = zr[phase][z].astype(F32)
        loop(Z - 1, receive)

    def z_start_up(phase):
        blocks, rows = PHASES[phase]

        def spread(step):
            flat[at(step, 16, 16), :] = yr[phase][step // blocks, step % blocks].astype(F32)

        loop(G * blocks, spread)
        z_start(phase, lambda to: flat[pl.ds(to, rows, stride=Z), :].astype(BF16))

    def z_start_back(phase):
        rows = PHASES[phase][1]
        z_start(phase, lambda to: flat[at(to * (rows // 16), rows, 16), :].astype(BF16))

    def y_start_back(phase):
        blocks, rows = PHASES[phase]

        def body(step):
            ys[phase][step // blocks, step % blocks] = flat[pl.ds(step, Z, stride=rows), :].astype(BF16)

        loop(G * blocks, body)
        y_start(phase)

    def split(part):
        first, count = part
        return lambda step: (step // count, first + step % count, step % count)

    def turn_up(phase, part):
        blocks, rows = PHASES[phase]

        def body(step):
            yy, row, own = split(part)(step)
            pieces = [
                flat[pl.ds((yy * 2 + hh) * blocks + own * 3 + b, Z, stride=rows), :]
                for b in range(3)
                for hh in range(2)
            ]
            pieces.append(jnp.zeros((32, C), F32))
            turned[at(yy * 3 + row, C, C), :] = jnp.concatenate(pieces, axis=0).T

        loop(Y * part[1], body)

    def turn_back(phase, part):
        blocks, rows = PHASES[phase]

        def body(step):
            yy, row, own = split(part)(step)
            values = turned[at(yy * 3 + row, C, C), :].T
            for b in range(3):
                for hh in range(2):
                    first = b * 32 + hh * 16
                    flat[pl.ds((yy * 2 + hh) * blocks + own * 3 + b, Z, stride=rows), :] = values[
                        first : first + 16
                    ]

        loop(Y * part[1], body)

    def low_columns(low):
        return at(low, C, C)

    def matrix(write):
        def body(low):
            write(low_columns(low), turned[pl.ds(low, ROWS, stride=8), :].astype(BF16))

        loop(8, body)

    def from_matrix(make):
        def body(low):
            turned[pl.ds(low, ROWS, stride=8), :] = make(low_columns(low))

        loop(8, body)

    def s_copy(phase, src, dst, slot, to):
        return pltpu.make_async_remote_copy(
            src_ref=src,
            dst_ref=dst,
            send_sem=s_send.at[phase, to],
            recv_sem=s_recv.at[phase, slot],
            device_id=shared(to),
            device_id_type=MESH,
        )

    def share(phase, ref):
        s_copy(phase, ref.at[s], ref.at[s], s, mate(1)).start()
        s_copy(phase, ref.at[s], ref.at[s], s, mate(0)).start()

    def passing_on(phase, ref):
        return pltpu.make_async_remote_copy(
            src_ref=ref.at[mate(1)],
            dst_ref=ref.at[mate(1)],
            send_sem=s_send.at[phase, mate(2)],
            recv_sem=s_recv.at[phase, mate(1)],
            device_id=shared(mate(0)),
            device_id_type=MESH,
        )

    def s_wait(phase, ref, slot):
        s_copy(phase, ref.at[slot], ref.at[slot], slot, slot).wait_recv()

    def pass_on(phase, ref):
        s_wait(phase, ref, mate(1))
        passing_on(phase, ref).start()

    def summing(which, rows):
        a_s, a_r, b_s, b_r, c_s, c_r, d_s, d_r, e_r = sums[which]
        sems = w_sems[which]

        def copy(step, src, dst, to, slot, device):
            return pltpu.make_async_remote_copy(
                src_ref=src,
                dst_ref=dst,
                send_sem=sems[2 * step].at[to],
                recv_sem=sems[2 * step + 1].at[slot],
                device_id=device,
                device_id_type=MESH,
            )

        copies = (
            lambda to, slot: copy(0, a_s.at[to], a_r.at[slot], to, slot, group(to)),
            lambda to, slot: copy(1, b_s.at[to], b_r.at[slot], to, slot, shared(to)),
            lambda to, slot: copy(2, c_s, c_r.at[slot], to, slot, along(to)),
            lambda to, slot: copy(3, d_s, d_r.at[slot], to, slot, shared(to)),
            lambda to, slot: copy(4, d_r, e_r.at[slot], to, slot, group(to)),
        )
        others = ((G - 1, next_g), (S - 1, mate), (Z - 1, next_z), (S - 1, mate), (G - 1, next_g))
        mine = (g, s, z, s, g)

        def start(step):
            count, other = others[step]
            loop(count, lambda d: copies[step](other(d), mine[step]).start())

        def wait(step):
            count, other = others[step]
            loop(count, lambda d: copies[step](other(d), other(d)).wait_recv())

        def first():
            start(0)
            a_r[g] = a_s[g]

        def second():
            wait(0)
            total = sum(a_r[k].astype(F32) for k in range(G))
            for k in range(S):
                b_s[k] = total[k * (rows // S) : (k + 1) * (rows // S)]
            start(1)
            b_r[s] = b_s[s]

        def third():
            wait(1)
            c_s[...] = sum(b_r[k] for k in range(S))
            start(2)
            c_r[z] = c_s[...]

        def fourth():
            wait(2)
            d_s[...] = sum(c_r[k] for k in range(Z)) * (1.0 / 768.0)
            start(3)
            d_r[s] = d_s[...]

        def fifth():
            wait(3)
            start(4)
            e_r[g] = d_r[...]

        def last(write):
            wait(4)
            for k in range(G):
                write(k, e_r[k].reshape(rows, C))

        def sent():
            for step, (count, other) in enumerate(others):
                loop(count, lambda d, c=copies[step], o=other: c(o(d), o(d)).wait_send())

        return first, second, third, fourth, fifth, last, sent

    for m in range(6):
        wt[m * C : (m + 1) * C] = weights_ref[m].astype(F32).T.astype(BF16)
    for m in range(5):
        wback[:, m * C : (m + 1) * C] = weights_ref[m]
    gwin[...] = jnp.zeros_like(gwin)

    def tile_rows(ref, row):
        return ref[at(row, TILE_ROWS, TILE_ROWS), :].astype(F32).reshape(16, 24, C)

    def block_of(values, b):
        return values[:, b * 8 : b * 8 + 8, :].reshape(C, C).T

    def rows_of(blocks):
        return jnp.concatenate([b.T.reshape(16, 8, C) for b in blocks], axis=1).reshape(TILE_ROWS, C)

    load_pair.wait()

    def project(row):
        values = tile_rows(pair_v, row)
        for b in range(3):
            block = row * 3 + b
            normed, inverse = normalize(block_of(values, b))
            rounded = normed.astype(BF16)
            xn[block] = normed
            xb[block] = rounded
            inv[block] = inverse
            p = nn(wt[: 5 * C], rounded)
            proj[block] = p
            mask = mask_ref[block]
            left_act = (mask * jax.nn.sigmoid(p[C : 2 * C]) * p[:C]).astype(BF16)
            right_act = (mask * jax.nn.sigmoid(p[3 * C : 4 * C]) * p[2 * C : 3 * C]).astype(BF16)
            for k in range(G):
                ys[LEFT][k, block] = left_act[k * 16 : k * 16 + 16]
                ys[RIGHT][k, block] = right_act[k * 16 : k * 16 + 16]

    loop(3, project)
    pl.semaphore_wait(barrier, Z + G + S - 3)

    whole = (0, 3)
    y_start(RIGHT)
    y_wait(RIGHT)
    y_start(LEFT)
    flat[G * BLOCKS * Z :, :] = jnp.zeros((8 * Z, C), F32)
    z_start_up(RIGHT)
    y_wait(LEFT)
    z_start_up(LEFT)

    def write_to(ref, *index):
        def write(columns, value):
            ref[(*index, slice(None), columns)] = value

        return write

    z_wait(RIGHT)
    turn_up(RIGHT, whole)
    matrix(write_to(right, s))
    share(0, right)
    load_cot.wait()
    load_order.wait()
    pass_on(0, right)
    z_wait(LEFT)
    turn_up(LEFT, whole)
    matrix(write_to(left, s))

    def triangle(part):
        tri[part, :, :ROWS] = nt(left[s], right[part]).astype(BF16)

    triangle(s)
    triangle(mate(1))
    s_wait(0, right, mate(0))
    triangle(mate(0))
    s_wait(0, right, mate(2))
    triangle(mate(2))
    from_matrix(
        lambda columns: sum(nn(tri[k, :, :ROWS], order[k, :, columns]) for k in range(S))
    )
    for part, phase in enumerate((TRI0, TRI1)):
        turn_back(phase, PARTS[part])
        z_start_back(phase)
    share(1, left)

    def tile(phase, back, part):
        def body(step):
            row = part[0] + step
            cotangent = tile_rows(cot_v, row)
            updates = []
            for b in range(3):
                block, own = row * 3 + b, step * 3 + b
                values = jnp.concatenate([yr[phase][k, own] for k in range(G)], axis=0)
                normed, inverse = normalize(values.astype(F32))
                rounded = normed.astype(BF16)
                linear = nn(wt[5 * C :], rounded)
                gate = jax.nn.sigmoid(proj[block, 4 * C :])
                updates.append(gate * linear)
                upstream = block_of(cotangent, b)
                grad_linear = (upstream * gate).astype(BF16)
                logit = (upstream * linear * gate * (1.0 - gate)).astype(BF16)
                stack[block, 4 * C :] = logit
                gwin[:, 4 * C : 5 * C] += nt(xb[block], logit)
                gwin[:, 5 * C :] += nt(rounded, grad_linear)
                grad_xout = nn(weights_ref[5], grad_linear)
                grad = norm_backward(grad_xout, normed, inverse).astype(BF16)
                for k in range(G):
                    ys[back][k, own] = grad[k * 16 : k * 16 + 16]
            upd_v[at(row, TILE_ROWS, TILE_ROWS), :] = rows_of(updates).astype(BF16)

        loop(part[1], body)

    z_wait(TRI0)
    y_start_back(TRI0)
    y_wait(TRI0)
    tile(TRI0, GRAD0, PARTS[0])
    y_start(GRAD0)
    z_wait(TRI1)
    y_start_back(TRI1)
    y_wait(GRAD0)
    z_start_up(GRAD0)
    y_wait(TRI1)
    tile(TRI1, GRAD1, PARTS[1])
    y_start(GRAD1)
    store_upd = pltpu.make_async_copy(upd_v, upd_hbm, local.at[0])
    store_upd.start()
    early = summing(0, 32)
    for k in range(G):
        m, first = 4 + k // 4, (k % 4) * 32
        sums[0][0][k] = gwin[first : first + 32, m * C : (m + 1) * C].astype(BF16)
    y_wait(GRAD1)
    z_start_up(GRAD1)
    early[0]()
    pass_on(1, left)
    z_wait(GRAD0)
    turn_up(GRAD0, PARTS[0])
    early[1]()
    z_wait(GRAD1)
    turn_up(GRAD1, PARTS[1])
    matrix(write_to(gmat))

    def columns_of(part):
        gts[part, :, :ROWS] = nt(order[part], gmat[...]).astype(BF16)

    loop(S, columns_of)

    def give(d):
        return s_copy(2, gts.at[mate(d)], gtr.at[s], s, mate(d))

    loop(S - 1, lambda d: give(d).start())
    gtr[s] = gts[s]

    def rows_for(part):
        gs[part, :, :ROWS] = nt(gmat[...], order[part]).astype(BF16)

    loop(S, rows_for)
    from_matrix(
        lambda columns: sum(nn(gs[k, :, :ROWS], right[k, :, columns]) for k in range(S))
    )
    turn_back(BACK_L, whole)
    z_start_back(BACK_L)
    early[2]()
    s_wait(1, left, mate(0))
    s_wait(1, left, mate(2))
    loop(S - 1, lambda d: s_wait(2, gtr, mate(d)))
    from_matrix(
        lambda columns: sum(nn(gtr[k, :, :ROWS], left[k, :, columns]) for k in range(S))
    )
    turn_back(BACK_R, whole)
    z_start_back(BACK_R)
    early[3]()

    def grads_of(phase, array):
        def body(block):
            values = jnp.concatenate([yr[phase][k, block] for k in range(G)], axis=0)
            upstream = values.astype(F32) * mask_ref[block]
            first = 2 * array * C
            value = proj[block, first : first + C]
            gate = jax.nn.sigmoid(proj[block, first + C : first + 2 * C])
            pieces = (upstream * gate, upstream * value * gate * (1.0 - gate))
            for k in range(2):
                piece = pieces[k].astype(BF16)
                columns = slice(first + k * C, first + (k + 1) * C)
                stack[block, columns] = piece
                gwin[:, columns] += nt(xb[block], piece)

        loop(BLOCKS, body)

    z_wait(BACK_L)
    y_start_back(BACK_L)
    early[4]()
    y_wait(BACK_L)
    grads_of(BACK_L, 0)

    def write_early(k, rows):
        gw_ref[4 + k // 4, (k % 4) * 32 : (k % 4) * 32 + 32] = rows

    early[5](write_early)
    z_wait(BACK_R)
    y_start_back(BACK_R)
    y_wait(BACK_R)
    grads_of(BACK_R, 1)
    late = summing(1, 64)
    for k in range(G):
        m, first = k // 2, (k % 2) * 64
        sums[1][0][k] = gwin[first : first + 64, m * C : (m + 1) * C].astype(BF16)
    late[0]()

    def store_gpair(row):
        rows = at(row, TILE_ROWS, TILE_ROWS)
        return pltpu.make_async_copy(gpair_v.at[rows], gpair_hbm.at[rows], local.at[3 + row])

    def finish(row):
        grads = []
        for b in range(3):
            block = row * 3 + b
            grads.append(norm_backward(nn(wback[...], stack[block]), xn[block], inv[block]))
        gpair_v[at(row, TILE_ROWS, TILE_ROWS), :] = rows_of(grads)
        store_gpair(row).start()

    loop(3, finish)
    for step in range(1, 5):
        late[step]()

    def write_late(k, rows):
        gw_ref[k // 2, (k % 2) * 64 : (k % 2) * 64 + 64] = rows

    late[5](write_late)

    store_upd.wait()
    loop(3, lambda row: store_gpair(row).wait())
    for phase in range(len(PHASES)):
        loop(G - 1, lambda d, p=phase: y_copy(p, next_g(d), g).wait_send())
        loop(Z - 1, lambda d, p=phase: z_copy(p, next_z(d), z).wait_send())
    for phase, ref in enumerate((right, left)):
        for d in range(2):
            s_copy(phase, ref.at[s], ref.at[s], s, mate(d)).wait_send()
        passing_on(phase, ref).wait_send()
    loop(S - 1, lambda d: give(d).wait_send())
    early[6]()
    late[6]()


def on_device(pair, pair_mask, weights, cotangent):
    pixels = pair.shape[0] * pair.shape[1]
    mask = pair_mask.astype(F32).reshape(3, 16, 3, 8).transpose(0, 2, 1, 3).reshape(BLOCKS, 1, C)
    vmem = pl.BlockSpec(memory_space=pltpu.VMEM)
    anywhere = pl.BlockSpec(memory_space=pl.ANY)

    def sems(*shape):
        return [pltpu.SemaphoreType.DMA(shape)] * 2

    def sum_buffers(rows):
        small = rows // S
        return [
            *[pltpu.VMEM((G, rows, C), BF16)] * 2,
            *[pltpu.VMEM((S, small, C), F32)] * 2,
            pltpu.VMEM((small, C), F32),
            pltpu.VMEM((Z, small, C), F32),
            pltpu.VMEM((small, C), F32),
            pltpu.VMEM((S, small, C), F32),
            pltpu.VMEM((G, S, small, C), F32),
        ]

    y_buffers = [pltpu.VMEM((G, blocks, 16, C), BF16) for blocks, _ in PHASES]
    z_buffers = [pltpu.VMEM((Z, rows, C), BF16) for _, rows in PHASES]
    update, grad_pair, grad_weights = pl.pallas_call(
        kernel,
        out_shape=(
            jax.ShapeDtypeStruct((pixels, C), BF16),
            jax.ShapeDtypeStruct((pixels, C), F32),
            jax.ShapeDtypeStruct((6, C, C), F32),
        ),
        in_specs=[anywhere] * 3 + [vmem] * 2,
        out_specs=(anywhere, anywhere, vmem),
        scratch_shapes=[
            pltpu.VMEM((pixels, C), BF16),
            pltpu.VMEM((pixels, C), BF16),
            pltpu.VMEM((S, ROWS, WIDE), BF16),
            pltpu.VMEM((pixels, C), BF16),
            pltpu.VMEM((pixels, C), F32),
            pltpu.VMEM((6 * C, C), BF16),
            pltpu.VMEM((C, 5 * C), BF16),
            pltpu.VMEM((BLOCKS, 5 * C, C), F32),
            pltpu.VMEM((BLOCKS, C, C), F32),
            pltpu.VMEM((BLOCKS, C, C), BF16),
            pltpu.VMEM((BLOCKS, 1, C), F32),
            pltpu.VMEM((BLOCKS, 5 * C, C), BF16),
            pltpu.VMEM((Z * 80, C), F32),
            pltpu.VMEM((12 * C, C), F32),
            pltpu.VMEM((S, ROWS, WIDE), BF16),
            pltpu.VMEM((S, ROWS, WIDE), BF16),
            pltpu.VMEM((ROWS, WIDE), BF16),
            *[pltpu.VMEM((S, ROWS, 256), BF16)] * 4,
            pltpu.VMEM((C, 6 * C), F32),
            *y_buffers,
            *y_buffers,
            *z_buffers,
            *z_buffers,
            *sum_buffers(32),
            *sum_buffers(64),
            *sems(len(PHASES), G),
            *sems(len(PHASES), Z),
            *sems(3, S),
            *[sem for _ in range(2) for n in (G, S, Z, S, G) for sem in sems(n)],
            pltpu.SemaphoreType.DMA((6,)),
        ],
        compiler_params=pltpu.CompilerParams(
            collective_id=0, has_side_effects=True, vmem_limit_bytes=56 * 1024 * 1024
        ),
    )(
        pair.reshape(pixels, C),
        cotangent.reshape(pixels, C),
        jnp.asarray(column_order()),
        mask,
        weights,
    )
    return update.reshape(pair.shape), grad_pair.reshape(pair.shape), grad_weights


def solution(mesh):
    placed = (P("row", "col", None), P("row", "col"), P(), P("row", "col", None))
    return jax.shard_map(
        on_device,
        mesh=mesh,
        in_specs=placed,
        out_specs=(P("row", "col", None), P("row", "col", None), P()),
        check_vma=False,
    )
```

```python
import jax
import jax.numpy as jnp
import numpy as np
from jax import lax
from jax.experimental import pallas as pl
from jax.experimental.pallas import tpu as pltpu
from jax.sharding import PartitionSpec as P


F32 = jnp.float32
BF16 = jnp.bfloat16
C = 128
BLOCKS = 9
Y, S, Z, G = 4, 4, 16, 8
ROWS = 192
WIDE = 1024
TILE_ROWS = 384
MESH = pl.DeviceIdType.MESH
RIGHT, LEFT, TRI, GRAD, BACK_L, BACK_R = range(6)
A0, A1, A2, T0, T1, G0, G1, B0, B1, B2 = range(10)


def some(array, first, last):
    return tuple((array, block) for block in range(first, last))


PHASES = (
    some(RIGHT, 0, 4),
    some(RIGHT, 4, 9) + some(LEFT, 8, 9),
    some(LEFT, 0, 8),
    some(TRI, 0, 6),
    some(TRI, 6, 9),
    some(GRAD, 0, 6),
    some(GRAD, 6, 9),
    some(BACK_L, 0, 8),
    some(BACK_L, 8, 9) + some(BACK_R, 0, 5),
    some(BACK_R, 5, 9),
)
WHERE = {item: (phase, k) for phase, items in enumerate(PHASES) for k, item in enumerate(items)}
HELD = tuple((len(items) * 8 + 15) // 16 * 16 for items in PHASES)


def nt(a, b):
    return lax.dot_general(a, b, (((1,), (1,)), ((), ())), preferred_element_type=F32)


def nn(a, b):
    return lax.dot_general(a, b, (((1,), (0,)), ((), ())), preferred_element_type=F32)


def tn(a, b):
    return lax.dot_general(a, b, (((0,), (0,)), ((), ())), preferred_element_type=F32)


def normalize(values):
    average = jnp.mean(values, axis=0, keepdims=True)
    centred = values - average
    variance = jnp.mean(centred * centred, axis=0, keepdims=True)
    inverse = lax.rsqrt(variance + 1e-05)
    return centred * inverse, inverse


def norm_backward(upstream, normed, inverse):
    first = jnp.mean(upstream, axis=0, keepdims=True)
    second = jnp.mean(upstream * normed, axis=0, keepdims=True)
    return inverse * (upstream - first - normed * second)


def column_order():
    low, block, tile = np.meshgrid(np.arange(8), np.arange(3), np.arange(32), indexing="ij")
    residue = (tile * 24 + block * 8 + low).reshape(-1)
    place = (low * 128 + block * 32 + tile).reshape(-1)
    y, s, inner = residue // 192, residue // 48 % 4, residue % 48
    order = np.zeros((S, ROWS, WIDE), np.float32)
    order[s, y * 48 + inner, place] = 1
    return order.astype(jnp.bfloat16)


def loop(count, body):
    def step(i, carry):
        body(i)
        return carry

    lax.fori_loop(0, count, step, 0)


def at(start, size, unit=8):
    return pl.ds(pl.multiple_of(start * unit, unit), size)


def kernel(
    pair_hbm,
    cot_hbm,
    order_hbm,
    mask_ref,
    weights_ref,
    upd_hbm,
    gpair_hbm,
    gw_ref,
    pair_v,
    cot_v,
    order,
    upd_v,
    gpair_v,
    wt,
    wback,
    proj,
    xn,
    xb,
    inv,
    stack,
    act,
    picked,
    turned,
    left,
    right,
    permuted,
    gmat,
    tri,
    gs,
    gts,
    gtr,
    gwin,
    *rest,
):
    rest = list(rest)
    ys, yr, zs, zr, flats = ([rest.pop(0) for _ in PHASES] for _ in range(5))
    sums = [[rest.pop(0) for _ in range(8)] for _ in range(3)]
    y_send, y_recv, z_send, z_recv, s_send, s_recv = (rest.pop(0) for _ in range(6))
    w_sems = [[rest.pop(0) for _ in range(8)] for _ in range(3)]
    local = rest.pop(0)

    r = lax.axis_index("row")
    q = lax.axis_index("col")
    y, s = r // 4, r % 4
    half, z = q // 16, q % 16
    g = y * 2 + half

    def group(other):
        return {"row": (other // 2) * 4 + s, "col": (other % 2) * 16 + z}

    def along(other):
        return {"row": r, "col": half * 16 + other}

    def mate(d):
        return ((s // 2 + (d + 1) // 2) % 2) * 2 + (s % 2 + (d + 1) % 2) % 2

    def shared(other):
        return {"row": y * 4 + other, "col": q}

    def next_g(d):
        return (g + 1 + d) % G

    def next_z(step):
        t = Z - 1 - step
        hop = ((t + 1) // 2) * (2 * (t % 2) - 1)
        return (z + hop + Z) % Z

    barrier = pltpu.get_barrier_semaphore()

    def greet(device):
        pl.semaphore_signal(barrier, inc=1, device_id=device, device_id_type=MESH)

    loop(Z - 1, lambda d: greet(along(next_z(d))))
    loop(G - 1, lambda d: greet(group(next_g(d))))
    loop(S - 1, lambda d: greet(shared(mate(d))))

    load_pair = pltpu.make_async_copy(pair_hbm, pair_v, local.at[0])
    load_cot = pltpu.make_async_copy(cot_hbm, cot_v, local.at[1])
    load_order = pltpu.make_async_copy(order_hbm, order, local.at[2])
    load_pair.start()
    load_cot.start()
    load_order.start()

    def y_copy(phase, to, slot):
        return pltpu.make_async_remote_copy(
            src_ref=ys[phase].at[to],
            dst_ref=yr[phase].at[slot],
            send_sem=y_send.at[phase, to],
            recv_sem=y_recv.at[phase, slot],
            device_id=group(to),
            device_id_type=MESH,
        )

    def y_start(phase):
        loop(G - 1, lambda d: y_copy(phase, next_g(d), g).start())
        yr[phase][g] = ys[phase][g]

    def y_wait(phase):
        loop(G - 1, lambda d: y_copy(phase, next_g(d), next_g(d)).wait_recv())

    def z_copy(phase, to, slot):
        return pltpu.make_async_remote_copy(
            src_ref=zs[phase].at[to],
            dst_ref=zr[phase].at[slot],
            send_sem=z_send.at[phase, to],
            recv_sem=z_recv.at[phase, slot],
            device_id=along(to),
            device_id_type=MESH,
        )

    def z_start(phase, make):
        def send(step):
            to = next_z(step)
            zs[phase][to] = make(to)
            z_copy(phase, to, z).start()

        loop(Z - 1, send)
        zr[phase][z] = make(z)

    def z_wait(phase):
        rows = HELD[phase]
        flat = flats[phase]

        def receive(step):
            frm = next_z(Z - 2 - step)
            z_copy(phase, frm, frm).wait_recv()
            flat[at(frm * (rows // 16), rows, 16), :] = zr[phase][frm].astype(F32)

        flat[at(z * (rows // 16), rows, 16), :] = zr[phase][z].astype(F32)
        loop(Z - 1, receive)

    def y_fill(phase):
        for k, (array, block) in enumerate(PHASES[phase]):
            for other in range(G):
                ys[phase][other, k] = act[array, block, other * 16 : other * 16 + 16]

    def z_start_up(phase):
        blocks, rows = len(PHASES[phase]), HELD[phase]

        def spread(step):
            picked[at(step, 16, 16), :] = yr[phase][step // blocks, step % blocks].astype(F32)

        loop(G * blocks, spread)
        z_start(phase, lambda to: picked[pl.ds(to, rows, stride=Z), :].astype(BF16))

    def z_start_back(phase):
        rows = HELD[phase]
        z_start(phase, lambda to: flats[phase][at(to * (rows // 16), rows, 16), :].astype(BF16))

    def y_start_back(phase):
        blocks, rows = len(PHASES[phase]), HELD[phase]

        def body(step):
            values = flats[phase][pl.ds(step, Z, stride=rows), :]
            ys[phase][step // blocks, step % blocks] = values.astype(BF16)

        loop(G * blocks, body)
        y_start(phase)

    def place(array, block, part):
        phase, k = WHERE[array, block]
        return flats[phase], pl.ds(part * len(PHASES[phase]) + k, Z, stride=HELD[phase])

    def turn_up(array, rows):
        for row in rows:

            def body(yy, row=row):
                pieces = []
                for b in range(3):
                    for hh in range(2):
                        flat, held = place(array, row * 3 + b, yy * 2 + hh)
                        pieces.append(flat[held, :])
                pieces.append(jnp.zeros((32, C), F32))
                turned[at(yy * 3 + row, C, C), :] = jnp.concatenate(pieces, axis=0).T

            loop(Y, body)

    def turn_back(array, rows):
        for row in rows:

            def body(yy, row=row):
                values = turned[at(yy * 3 + row, C, C), :].T
                for b in range(3):
                    for hh in range(2):
                        first = b * 32 + hh * 16
                        flat, held = place(array, row * 3 + b, yy * 2 + hh)
                        flat[held, :] = values[first : first + 16]

            loop(Y, body)

    def low_columns(low):
        return at(low, C, C)

    def matrix(write):
        def body(low):
            write(low_columns(low), turned[pl.ds(low, ROWS, stride=8), :].astype(BF16))

        loop(8, body)

    def from_matrix(make):
        def body(low):
            turned[pl.ds(low, ROWS, stride=8), :] = make(low_columns(low))

        loop(8, body)

    def s_copy(phase, src, dst, slot, to):
        return pltpu.make_async_remote_copy(
            src_ref=src,
            dst_ref=dst,
            send_sem=s_send.at[phase, to],
            recv_sem=s_recv.at[phase, slot],
            device_id=shared(to),
            device_id_type=MESH,
        )

    def share(phase, ref):
        s_copy(phase, ref.at[s], ref.at[s], s, mate(1)).start()
        s_copy(phase, ref.at[s], ref.at[s], s, mate(0)).start()

    def passing_on(phase, ref):
        return pltpu.make_async_remote_copy(
            src_ref=ref.at[mate(1)],
            dst_ref=ref.at[mate(1)],
            send_sem=s_send.at[phase, mate(2)],
            recv_sem=s_recv.at[phase, mate(1)],
            device_id=shared(mate(0)),
            device_id_type=MESH,
        )

    def s_wait(phase, ref, slot):
        s_copy(phase, ref.at[slot], ref.at[slot], slot, slot).wait_recv()

    def pass_on(phase, ref):
        s_wait(phase, ref, mate(1))
        passing_on(phase, ref).start()

    def summing(which, first):
        a_s, a_r, b_s, b_r, c_s, c_r, d_s, d_r = sums[which]
        sems = w_sems[which]

        def copy(step, src, dst, to, slot, device):
            return pltpu.make_async_remote_copy(
                src_ref=src,
                dst_ref=dst,
                send_sem=sems[2 * step].at[to],
                recv_sem=sems[2 * step + 1].at[slot],
                device_id=device,
                device_id_type=MESH,
            )

        copies = (
            lambda to, slot: copy(0, a_s.at[to], a_r.at[slot], to, slot, along(to)),
            lambda to, slot: copy(1, b_s, b_r.at[slot], to, slot, group(to)),
            lambda to, slot: copy(2, c_s, c_r.at[slot], to, slot, shared(to)),
            lambda to, slot: copy(3, d_s, d_r.at[slot], to, slot, along(to)),
        )
        others = ((Z - 1, next_z), (G - 1, next_g), (S - 1, mate), (Z - 1, next_z))
        mine = (z, g, s, z)

        def start(step):
            count, other = others[step]
            loop(count, lambda d: copies[step](other(d), mine[step]).start())

        def wait(step):
            count, other = others[step]
            loop(count, lambda d: copies[step](other(d), other(d)).wait_recv())

        def one():
            for k in range(Z):
                rows, columns = (k % 8) * 16, (first + k // 8) * C
                a_s[k] = gwin[rows : rows + 16, columns : columns + C].astype(BF16)
            start(0)
            a_r[z] = a_s[z]

        def two():
            wait(0)
            b_s[...] = sum(a_r[k].astype(F32) for k in range(Z))
            start(1)
            b_r[g] = b_s[...]

        def three():
            wait(1)
            c_s[...] = sum(b_r[k] for k in range(G))
            start(2)
            c_r[s] = c_s[...]

        def four():
            wait(2)
            d_s[...] = (sum(c_r[k] for k in range(S)) * (1.0 / 768.0)).astype(BF16)
            start(3)
            d_r[z] = d_s[...]

        def five():
            wait(3)
            for k in range(Z):
                gw_ref[first + k // 8, (k % 8) * 16 : (k % 8) * 16 + 16] = d_r[k].astype(F32)

        def sent():
            for step, (count, other) in enumerate(others):
                loop(count, lambda d, c=copies[step], o=other: c(o(d), o(d)).wait_send())

        return one, two, three, four, five, sent

    for m in range(6):
        wt[m * C : (m + 1) * C] = weights_ref[m].astype(F32).T.astype(BF16)
    for m in range(5):
        wback[:, m * C : (m + 1) * C] = weights_ref[m]
    gwin[...] = jnp.zeros_like(gwin)

    def tile_rows(ref, row):
        return ref[at(row, TILE_ROWS, TILE_ROWS), :].astype(F32).reshape(16, 24, C)

    def block_of(values, b):
        return values[:, b * 8 : b * 8 + 8, :].reshape(C, C).T

    def rows_of(blocks):
        return jnp.concatenate([b.T.reshape(16, 8, C) for b in blocks], axis=1).reshape(TILE_ROWS, C)

    load_pair.wait()

    def activate(block, array):
        first = 2 * array * C
        p = nn(wt[first : first + 2 * C], xb[block])
        proj[block, first : first + 2 * C] = p
        value = mask_ref[block] * jax.nn.sigmoid(p[C:]) * p[:C]
        act[RIGHT if array else LEFT, block] = value.astype(BF16)

    def project_right(row):
        values = tile_rows(pair_v, row)
        for b in range(3):
            block = row * 3 + b
            normed, inverse = normalize(block_of(values, b))
            xn[block] = normed
            xb[block] = normed.astype(BF16)
            inv[block] = inverse
            activate(block, 1)

    def project_gate(block):
        proj[block, 4 * C :] = jax.nn.sigmoid(nn(wt[4 * C : 5 * C], xb[block]))

    loop(3, project_right)
    y_fill(A0)
    pl.semaphore_wait(barrier, Z + G + S - 3)

    whole = range(3)
    y_start(A0)
    loop(BLOCKS, lambda block: activate(block, 0))
    y_fill(A1)
    y_start(A1)
    y_wait(A0)
    z_start_up(A0)
    y_fill(A2)
    y_wait(A1)
    y_start(A2)
    z_start_up(A1)
    y_wait(A2)
    z_start_up(A2)
    loop(BLOCKS, project_gate)

    def write_to(ref, *index):
        def write(columns, value):
            ref[(*index, slice(None), columns)] = value

        return write

    z_wait(A0)
    turn_up(RIGHT, range(1))
    z_wait(A1)
    turn_up(RIGHT, range(1, 3))
    matrix(write_to(right, s))
    share(0, right)
    load_cot.wait()
    load_order.wait()
    pass_on(0, right)
    z_wait(A2)
    turn_up(LEFT, whole)
    matrix(write_to(left, s))

    def triangle(part):
        tri[part, :, :ROWS] = nt(left[s], right[part]).astype(BF16)

    triangle(s)
    triangle(mate(1))
    s_wait(0, right, mate(0))
    triangle(mate(0))
    s_wait(0, right, mate(2))
    triangle(mate(2))
    from_matrix(
        lambda columns: sum(nn(tri[k, :, :ROWS], order[k, :, columns]) for k in range(S))
    )
    turn_back(TRI, range(2))
    z_start_back(T0)
    turn_back(TRI, range(2, 3))
    z_start_back(T1)
    share(1, left)

    def permute(low):
        rows = low_columns(low)
        permuted[rows, :] = sum(tn(order[k, :, rows], right[k]) for k in range(S)).astype(BF16)

    loop(8, permute)

    def tile(phase, first, count):
        def body(step):
            row = first + step
            cotangent = tile_rows(cot_v, row)
            updates = []
            for b in range(3):
                block, own = row * 3 + b, step * 3 + b
                values = jnp.concatenate([yr[phase][k, own] for k in range(G)], axis=0)
                normed, inverse = normalize(values.astype(F32))
                rounded = normed.astype(BF16)
                linear = nn(wt[5 * C :], rounded)
                gate = proj[block, 4 * C :]
                updates.append(gate * linear)
                upstream = block_of(cotangent, b)
                grad_linear = (upstream * gate).astype(BF16)
                logit = (upstream * linear * gate * (1.0 - gate)).astype(BF16)
                stack[block, 4 * C :] = logit
                gwin[:, 4 * C : 5 * C] += nt(xb[block], logit)
                gwin[:, 5 * C :] += nt(rounded, grad_linear)
                grad_xout = nn(weights_ref[5], grad_linear)
                grad = norm_backward(grad_xout, normed, inverse).astype(BF16)
                for k in range(G):
                    ys[phase + G0 - T0][k, own] = grad[k * 16 : k * 16 + 16]
            upd_v[at(row, TILE_ROWS, TILE_ROWS), :] = rows_of(updates).astype(BF16)

        loop(count, body)

    z_wait(T0)
    y_start_back(T0)
    y_wait(T0)
    tile(T0, 0, 2)
    y_start(G0)
    z_wait(T1)
    y_start_back(T1)
    y_wait(G0)
    z_start_up(G0)
    y_wait(T1)
    tile(T1, 2, 1)
    y_start(G1)
    store_upd = pltpu.make_async_copy(upd_v, upd_hbm, local.at[0])
    store_upd.start()
    early = summing(0, 4)
    y_wait(G1)
    z_start_up(G1)
    early[0]()
    pass_on(1, left)
    z_wait(G0)
    turn_up(GRAD, range(2))
    z_wait(G1)
    turn_up(GRAD, range(2, 3))
    matrix(write_to(gmat))

    from_matrix(lambda columns: nn(gmat[...], permuted[:, columns]))
    turn_back(BACK_L, whole)
    z_start_back(B0)

    def columns_of(part):
        gts[part, :, :ROWS] = nt(order[part], gmat[...]).astype(BF16)

    loop(S, columns_of)

    def give(d):
        return s_copy(2, gts.at[mate(d)], gtr.at[s], s, mate(d))

    loop(S - 1, lambda d: give(d).start())
    gtr[s] = gts[s]
    early[1]()
    s_wait(1, left, mate(0))
    s_wait(1, left, mate(2))
    loop(S - 1, lambda d: s_wait(2, gtr, mate(d)))
    from_matrix(
        lambda columns: sum(nn(gtr[k, :, :ROWS], left[k, :, columns]) for k in range(S))
    )
    turn_back(BACK_R, whole)
    z_start_back(B1)
    z_start_back(B2)
    early[2]()

    def grads_of(array, phase, first, block_first, count):
        def body(step):
            block, own = block_first + step, first + step
            values = jnp.concatenate([yr[phase][k, own] for k in range(G)], axis=0)
            upstream = values.astype(F32) * mask_ref[block]
            row = 2 * array * C
            value = proj[block, row : row + C]
            gate = jax.nn.sigmoid(proj[block, row + C : row + 2 * C])
            pieces = (upstream * gate, upstream * value * gate * (1.0 - gate))
            for k in range(2):
                piece = pieces[k].astype(BF16)
                columns = slice(row + k * C, row + (k + 1) * C)
                stack[block, columns] = piece
                gwin[:, columns] += nt(xb[block], piece)

        loop(count, body)

    z_wait(B0)
    y_start_back(B0)
    early[3]()
    y_wait(B0)
    grads_of(0, B0, 0, 0, 8)
    z_wait(B1)
    y_start_back(B1)
    y_wait(B1)
    grads_of(0, B1, 0, 8, 1)
    middle = summing(1, 0)
    middle[0]()
    grads_of(1, B1, 1, 0, 5)
    z_wait(B2)
    y_start_back(B2)
    early[4]()
    middle[1]()
    y_wait(B2)
    grads_of(1, B2, 0, 5, 4)
    late = summing(2, 2)
    late[0]()
    middle[2]()

    def store_gpair(row):
        rows = at(row, TILE_ROWS, TILE_ROWS)
        return pltpu.make_async_copy(gpair_v.at[rows], gpair_hbm.at[rows], local.at[3 + row])

    def finish(row):
        grads = []
        for b in range(3):
            block = row * 3 + b
            grads.append(norm_backward(nn(wback[...], stack[block]), xn[block], inv[block]))
        gpair_v[at(row, TILE_ROWS, TILE_ROWS), :] = rows_of(grads)
        store_gpair(row).start()

    loop(3, finish)
    late[1]()
    middle[3]()
    late[2]()
    late[3]()
    middle[4]()
    late[4]()

    store_upd.wait()
    loop(3, lambda row: store_gpair(row).wait())
    for phase in range(len(PHASES)):
        loop(G - 1, lambda d, p=phase: y_copy(p, next_g(d), g).wait_send())
        loop(Z - 1, lambda d, p=phase: z_copy(p, next_z(d), z).wait_send())
    for phase, ref in enumerate((right, left)):
        for d in range(2):
            s_copy(phase, ref.at[s], ref.at[s], s, mate(d)).wait_send()
        passing_on(phase, ref).wait_send()
    loop(S - 1, lambda d: give(d).wait_send())
    early[5]()
    middle[5]()
    late[5]()


def on_device(pair, pair_mask, weights, cotangent):
    pixels = pair.shape[0] * pair.shape[1]
    mask = pair_mask.astype(F32).reshape(3, 16, 3, 8).transpose(0, 2, 1, 3).reshape(BLOCKS, 1, C)
    vmem = pl.BlockSpec(memory_space=pltpu.VMEM)
    anywhere = pl.BlockSpec(memory_space=pl.ANY)

    def sems(*shape):
        return [pltpu.SemaphoreType.DMA(shape)] * 2

    def sum_buffers():
        one = [pltpu.VMEM((16, C), F32), pltpu.VMEM((G, 16, C), F32)]
        two = [pltpu.VMEM((16, C), F32), pltpu.VMEM((S, 16, C), F32)]
        last = [pltpu.VMEM((16, C), BF16), pltpu.VMEM((Z, 16, C), BF16)]
        return [pltpu.VMEM((Z, 16, C), BF16)] * 2 + one + two + last

    y_buffers = [pltpu.VMEM((G, len(items), 16, C), BF16) for items in PHASES]
    z_buffers = [pltpu.VMEM((Z, rows, C), BF16) for rows in HELD]
    update, grad_pair, grad_weights = pl.pallas_call(
        kernel,
        out_shape=(
            jax.ShapeDtypeStruct((pixels, C), BF16),
            jax.ShapeDtypeStruct((pixels, C), F32),
            jax.ShapeDtypeStruct((6, C, C), F32),
        ),
        in_specs=[anywhere] * 3 + [vmem] * 2,
        out_specs=(anywhere, anywhere, vmem),
        scratch_shapes=[
            pltpu.VMEM((pixels, C), BF16),
            pltpu.VMEM((pixels, C), BF16),
            pltpu.VMEM((S, ROWS, WIDE), BF16),
            pltpu.VMEM((pixels, C), BF16),
            pltpu.VMEM((pixels, C), F32),
            pltpu.VMEM((6 * C, C), BF16),
            pltpu.VMEM((C, 5 * C), BF16),
            pltpu.VMEM((BLOCKS, 5 * C, C), F32),
            pltpu.VMEM((BLOCKS, C, C), F32),
            pltpu.VMEM((BLOCKS, C, C), BF16),
            pltpu.VMEM((BLOCKS, 1, C), F32),
            pltpu.VMEM((BLOCKS, 5 * C, C), BF16),
            pltpu.VMEM((2, BLOCKS, C, C), BF16),
            pltpu.VMEM((Z * max(HELD), C), F32),
            pltpu.VMEM((12 * C, C), F32),
            pltpu.VMEM((S, ROWS, WIDE), BF16),
            pltpu.VMEM((S, ROWS, WIDE), BF16),
            pltpu.VMEM((WIDE, WIDE), BF16),
            pltpu.VMEM((ROWS, WIDE), BF16),
            *[pltpu.VMEM((S, ROWS, 256), BF16)] * 4,
            pltpu.VMEM((C, 6 * C), F32),
            *y_buffers,
            *y_buffers,
            *z_buffers,
            *z_buffers,
            *[pltpu.VMEM((Z * rows, C), F32) for rows in HELD],
            *[buffer for _ in range(3) for buffer in sum_buffers()],
            *sems(len(PHASES), G),
            *sems(len(PHASES), Z),
            *sems(3, S),
            *[sem for _ in range(3) for n in (Z, G, S, Z) for sem in sems(n)],
            pltpu.SemaphoreType.DMA((6,)),
        ],
        compiler_params=pltpu.CompilerParams(
            collective_id=0, has_side_effects=True, vmem_limit_bytes=56 * 1024 * 1024
        ),
    )(
        pair.reshape(pixels, C),
        cotangent.reshape(pixels, C),
        jnp.asarray(column_order()),
        mask,
        weights,
    )
    return update.reshape(pair.shape), grad_pair.reshape(pair.shape), grad_weights


def solution(mesh):
    placed = (P("row", "col", None), P("row", "col"), P(), P("row", "col", None))
    return jax.shard_map(
        on_device,
        mesh=mesh,
        in_specs=placed,
        out_specs=(P("row", "col", None), P("row", "col", None), P()),
        check_vma=False,
    )
```

```python
import jax
import jax.numpy as jnp
import numpy as np
from jax import lax
from jax.experimental import pallas as pl
from jax.experimental.pallas import tpu as pltpu
from jax.sharding import PartitionSpec as P


F32 = jnp.float32
BF16 = jnp.bfloat16
C = 128
BLOCKS = 9
Y, S, Z, G = 4, 4, 16, 8
ROWS = 192
WIDE = 1024
TILE_ROWS = 384
MESH = pl.DeviceIdType.MESH
RIGHT, LEFT, TRI, GRAD, BACK_L, BACK_R = range(6)
A0, A1, A2, A3, T0, T1, T2, G0, G1, G2, B0, B1, B2, B3 = range(14)


def some(array, first, last):
    return tuple((array, block) for block in range(first, last))


PHASES = (
    some(RIGHT, 0, 6),
    some(RIGHT, 6, 9) + some(LEFT, 0, 1),
    some(LEFT, 1, 3),
    some(LEFT, 3, 9),
    some(TRI, 0, 2),
    some(TRI, 2, 6),
    some(TRI, 6, 9),
    some(GRAD, 0, 2),
    some(GRAD, 2, 6),
    some(GRAD, 6, 9),
    some(BACK_L, 0, 6),
    some(BACK_L, 6, 8),
    some(BACK_L, 8, 9) + some(BACK_R, 0, 5),
    some(BACK_R, 5, 9),
)
WHERE = {item: (phase, k) for phase, items in enumerate(PHASES) for k, item in enumerate(items)}
HELD = tuple((len(items) * 8 + 15) // 16 * 16 for items in PHASES)


def nt(a, b):
    return lax.dot_general(a, b, (((1,), (1,)), ((), ())), preferred_element_type=F32)


def nn(a, b):
    return lax.dot_general(a, b, (((1,), (0,)), ((), ())), preferred_element_type=F32)


def normalize(values):
    average = jnp.mean(values, axis=0, keepdims=True)
    centred = values - average
    variance = jnp.mean(centred * centred, axis=0, keepdims=True)
    inverse = lax.rsqrt(variance + 1e-05)
    return centred * inverse, inverse


def norm_backward(upstream, normed, inverse):
    first = jnp.mean(upstream, axis=0, keepdims=True)
    second = jnp.mean(upstream * normed, axis=0, keepdims=True)
    return inverse * (upstream - first - normed * second)


def column_order():
    low, block, tile = np.meshgrid(np.arange(8), np.arange(3), np.arange(32), indexing="ij")
    residue = (tile * 24 + block * 8 + low).reshape(-1)
    place = (low * 128 + block * 32 + tile).reshape(-1)
    y, s, inner = residue // 192, residue // 48 % 4, residue % 48
    order = np.zeros((S, ROWS, WIDE), np.float32)
    order[s, inner // 16 * 64 + y * 16 + inner % 16, place] = 1
    return order.astype(jnp.bfloat16)


def loop(count, body):
    def step(i, carry):
        body(i)
        return carry

    lax.fori_loop(0, count, step, 0)


def at(start, size, unit=8):
    return pl.ds(pl.multiple_of(start * unit, unit), size)


def kernel(
    pair_hbm,
    cot_hbm,
    order_hbm,
    mask_ref,
    weights_ref,
    upd_hbm,
    gpair_hbm,
    gw_ref,
    pair_v,
    cot_v,
    order,
    upd_v,
    gpair_v,
    wt,
    wback,
    proj,
    xn,
    xb,
    inv,
    stack,
    act,
    picked,
    turned,
    left,
    right,
    permuted,
    gmat,
    residues,
    gs,
    gts0,
    gtr0,
    gts1,
    gtr1,
    gwin,
    upstream,
    updates,
    *rest,
):
    rest = list(rest)
    ys, yr, zs, zr, flats = ([rest.pop(0) for _ in PHASES] for _ in range(5))
    sums = [[rest.pop(0) for _ in range(8)] for _ in range(3)]
    y_send, y_recv, z_send, z_recv, s_send, s_recv = (rest.pop(0) for _ in range(6))
    w_sems = [[rest.pop(0) for _ in range(8)] for _ in range(3)]
    local = rest.pop(0)

    r = lax.axis_index("row")
    q = lax.axis_index("col")
    y, s = r // 4, r % 4
    half, z = q // 16, q % 16
    g = y * 2 + half

    def group(other):
        return {"row": (other // 2) * 4 + s, "col": (other % 2) * 16 + z}

    def along(other):
        return {"row": r, "col": half * 16 + other}

    def mate(d):
        return ((s // 2 + (d + 1) // 2) % 2) * 2 + (s % 2 + (d + 1) % 2) % 2

    def shared(other):
        return {"row": y * 4 + other, "col": q}

    def next_g(d):
        return (g + 1 + d) % G

    def next_z(step):
        t = Z - 1 - step
        hop = ((t + 1) // 2) * (2 * (t % 2) - 1)
        return (z + hop + Z) % Z

    barrier = pltpu.get_barrier_semaphore()

    def greet(device):
        pl.semaphore_signal(barrier, inc=1, device_id=device, device_id_type=MESH)

    loop(Z - 1, lambda d: greet(along(next_z(d))))
    loop(G - 1, lambda d: greet(group(next_g(d))))
    loop(S - 1, lambda d: greet(shared(mate(d))))

    load_pair = pltpu.make_async_copy(pair_hbm, pair_v, local.at[0])
    load_cot = pltpu.make_async_copy(cot_hbm, cot_v, local.at[1])
    load_order = pltpu.make_async_copy(order_hbm, order, local.at[2])
    load_pair.start()
    load_cot.start()
    load_order.start()

    def y_copy(phase, to, slot):
        return pltpu.make_async_remote_copy(
            src_ref=ys[phase].at[to],
            dst_ref=yr[phase].at[slot],
            send_sem=y_send.at[phase, to],
            recv_sem=y_recv.at[phase, slot],
            device_id=group(to),
            device_id_type=MESH,
        )

    def y_start(phase):
        loop(G - 1, lambda d: y_copy(phase, next_g(d), g).start())
        yr[phase][g] = ys[phase][g]

    def y_wait(phase):
        loop(G - 1, lambda d: y_copy(phase, next_g(d), next_g(d)).wait_recv())

    def z_copy(phase, to, slot):
        return pltpu.make_async_remote_copy(
            src_ref=zs[phase].at[to],
            dst_ref=zr[phase].at[slot],
            send_sem=z_send.at[phase, to],
            recv_sem=z_recv.at[phase, slot],
            device_id=along(to),
            device_id_type=MESH,
        )

    def z_start(phase, make):
        def send(step):
            to = next_z(step)
            zs[phase][to] = make(to)
            z_copy(phase, to, z).start()

        loop(Z - 1, send)
        zr[phase][z] = make(z)

    def z_wait(phase):
        rows = HELD[phase]
        flat = flats[phase]

        def receive(step):
            frm = next_z(Z - 2 - step)
            z_copy(phase, frm, frm).wait_recv()

        def widen(step):
            for k in range(4):
                frm = step * 4 + k
                flat[at(frm * (rows // 16), rows, 16), :] = zr[phase][frm].astype(F32)

        loop(Z - 1, receive)
        loop(Z // 4, widen)

    def y_fill(phase):
        for k, (array, block) in enumerate(PHASES[phase]):
            for other in range(G):
                ys[phase][other, k] = act[array, block, other * 16 : other * 16 + 16]

    def z_start_up(phase):
        blocks, rows = len(PHASES[phase]), HELD[phase]

        def spread(k):
            for other in range(G):
                picked[at(other * blocks + k, 16, 16), :] = yr[phase][other, k].astype(F32)

        loop(blocks, spread)
        z_start(phase, lambda to: picked[pl.ds(to, rows, stride=Z), :].astype(BF16))

    def z_start_back(phase):
        rows = HELD[phase]
        z_start(phase, lambda to: flats[phase][at(to * (rows // 16), rows, 16), :].astype(BF16))

    def y_start_back(phase):
        blocks, rows = len(PHASES[phase]), HELD[phase]

        def body(k):
            for other in range(G):
                values = flats[phase][pl.ds(other * blocks + k, Z, stride=rows), :]
                ys[phase][other, k] = values.astype(BF16)

        loop(blocks, body)
        y_start(phase)

    def place(array, block, part):
        phase, k = WHERE[array, block]
        return flats[phase], pl.ds(part * len(PHASES[phase]) + k, Z, stride=HELD[phase])

    def turn_up(array, rows):
        for row in rows:

            for yy in range(Y):
                pieces = []
                for b in range(3):
                    for hh in range(2):
                        flat, spot = place(array, row * 3 + b, yy * 2 + hh)
                        pieces.append(flat[spot, :])
                pieces.append(jnp.zeros((32, C), F32))
                turned[(row * Y + yy) * C : (row * Y + yy + 1) * C, :] = jnp.concatenate(pieces, axis=0).T

    def turn_back(array, rows):
        for row in rows:

            for yy in range(Y):
                values = turned[(row * Y + yy) * C : (row * Y + yy + 1) * C, :].T
                for b in range(3):
                    for hh in range(2):
                        first = b * 32 + hh * 16
                        flat, spot = place(array, row * 3 + b, yy * 2 + hh)
                        flat[spot, :] = values[first : first + 16]

    def low_columns(low):
        return at(low, C, C)

    def held(rows):
        size = 64 * len(rows)
        return slice(rows[0] * 64, rows[0] * 64 + size), lambda low: pl.ds(
            rows[0] * 512 + low, size, stride=8
        )

    def matrix(ref, rows):
        kept, where = held(rows)

        def body(pair):
            for low in (2 * pair, 2 * pair + 1):
                ref[kept, low_columns(low)] = turned[where(low), :].astype(BF16)

        loop(4, body)

    def from_matrix(rows, make):
        kept, where = held(rows)

        def body(pair):
            values = make(kept, at(pair, 2 * C, 2 * C))
            turned[where(2 * pair), :] = values[:, :C]
            turned[where(2 * pair + 1), :] = values[:, C:]

        loop(4, body)

    def s_copy(phase, src, dst, slot, to):
        return pltpu.make_async_remote_copy(
            src_ref=src,
            dst_ref=dst,
            send_sem=s_send.at[phase, to],
            recv_sem=s_recv.at[phase, slot],
            device_id=shared(to),
            device_id_type=MESH,
        )

    def share(phase, ref, rows):
        part = ref.at[s, rows]
        s_copy(phase, part, part, s, mate(1)).start()
        s_copy(phase, part, part, s, mate(0)).start()

    def passing_on(phase, ref, rows):
        return pltpu.make_async_remote_copy(
            src_ref=ref.at[mate(1), rows],
            dst_ref=ref.at[mate(1), rows],
            send_sem=s_send.at[phase, mate(2)],
            recv_sem=s_recv.at[phase, mate(1)],
            device_id=shared(mate(0)),
            device_id_type=MESH,
        )

    def s_wait(phase, ref, slot, rows):
        part = ref.at[slot, rows]
        s_copy(phase, part, part, slot, slot).wait_recv()

    def pass_on(phase, ref, rows):
        s_wait(phase, ref, mate(1), rows)
        passing_on(phase, ref, rows).start()

    def summing(which, first):
        a_s, a_r, b_s, b_r, c_s, c_r, d_s, d_r = sums[which]
        sems = w_sems[which]

        def copy(step, src, dst, to, slot, device):
            return pltpu.make_async_remote_copy(
                src_ref=src,
                dst_ref=dst,
                send_sem=sems[2 * step].at[to],
                recv_sem=sems[2 * step + 1].at[slot],
                device_id=device,
                device_id_type=MESH,
            )

        copies = (
            lambda to, slot: copy(0, a_s.at[to], a_r.at[slot], to, slot, along(to)),
            lambda to, slot: copy(1, b_s, b_r.at[slot], to, slot, group(to)),
            lambda to, slot: copy(2, c_s, c_r.at[slot], to, slot, shared(to)),
            lambda to, slot: copy(3, d_s, d_r.at[slot], to, slot, along(to)),
        )
        others = ((Z - 1, next_z), (G - 1, next_g), (S - 1, mate), (Z - 1, next_z))
        mine = (z, g, s, z)

        def start(step):
            count, other = others[step]
            loop(count, lambda d: copies[step](other(d), mine[step]).start())

        def wait(step):
            count, other = others[step]
            loop(count, lambda d: copies[step](other(d), other(d)).wait_recv())

        def one():
            for k in range(Z):
                rows, columns = (k % 8) * 16, (first + k // 8) * C
                a_s[k] = gwin[rows : rows + 16, columns : columns + C].astype(BF16)
            start(0)
            a_r[z] = a_s[z]

        def two():
            wait(0)
            b_s[...] = sum(a_r[k].astype(F32) for k in range(Z))
            start(1)
            b_r[g] = b_s[...]

        def three():
            wait(1)
            c_s[...] = sum(b_r[k] for k in range(G))
            start(2)
            c_r[s] = c_s[...]

        def four():
            wait(2)
            d_s[...] = (sum(c_r[k] for k in range(S)) * (1.0 / 768.0)).astype(BF16)
            start(3)
            d_r[z] = d_s[...]

        def five():
            wait(3)
            for k in range(Z):
                gw_ref[first + k // 8, (k % 8) * 16 : (k % 8) * 16 + 16] = d_r[k].astype(F32)

        def sent():
            for step, (count, other) in enumerate(others):
                loop(count, lambda d, c=copies[step], o=other: c(o(d), o(d)).wait_send())

        return one, two, three, four, five, sent

    for m in range(6):
        wt[m * C : (m + 1) * C] = weights_ref[m].astype(F32).T.astype(BF16)
    for m in range(5):
        wback[:, m * C : (m + 1) * C] = weights_ref[m]
    gwin[...] = jnp.zeros_like(gwin)

    def tile_rows(ref, row):
        return ref[at(row, TILE_ROWS, TILE_ROWS), :].astype(F32).reshape(16, 24, C)

    def block_of(values, b):
        return values[:, b * 8 : b * 8 + 8, :].reshape(C, C).T

    def rows_of(blocks):
        return jnp.concatenate([b.T.reshape(16, 8, C) for b in blocks], axis=1).reshape(TILE_ROWS, C)

    load_pair.wait()

    def activate(block, array):
        first = 2 * array * C
        p = nn(wt[first : first + 2 * C], xb[block])
        proj[block, first : first + 2 * C] = p
        value = mask_ref[block] * jax.nn.sigmoid(p[C:]) * p[:C]
        act[RIGHT if array else LEFT, block] = value.astype(BF16)

    def project_right(row):
        values = tile_rows(pair_v, row)
        for b in range(3):
            block = row * 3 + b
            normed, inverse = normalize(block_of(values, b))
            xn[block] = normed
            xb[block] = normed.astype(BF16)
            inv[block] = inverse
            activate(block, 1)

    def project_gate(block):
        proj[block, 4 * C :] = jax.nn.sigmoid(nn(wt[4 * C : 5 * C], xb[block]))

    loop(3, project_right)
    y_fill(A0)
    pl.semaphore_wait(barrier, Z + G + S - 3)

    y_start(A0)
    loop(BLOCKS, lambda block: activate(block, 0))
    y_fill(A1)
    y_start(A1)
    y_fill(A2)
    y_fill(A3)
    y_wait(A0)
    z_start_up(A0)
    y_start(A2)
    y_wait(A1)
    z_start_up(A1)
    y_start(A3)
    y_wait(A2)
    z_start_up(A2)
    y_wait(A3)
    z_start_up(A3)
    loop(BLOCKS, project_gate)
    load_cot.wait()

    def turn_cotangent(row):
        values = tile_rows(cot_v, row)
        for b in range(3):
            upstream[row * 3 + b] = block_of(values, b)

    loop(3, turn_cotangent)
    load_order.wait()
    whole, two, last = range(3), range(2), range(2, 3)
    most, least, full = slice(0, 128), slice(128, 192), slice(0, 192)
    z_wait(A0)
    turn_up(RIGHT, two)
    matrix(right.at[s], two)
    share(0, right, most)
    z_wait(A1)
    turn_up(RIGHT, last)
    matrix(right.at[s], last)
    share(1, right, least)
    pass_on(0, right, most)
    z_wait(A2)
    turn_up(LEFT, range(1))
    matrix(left.at[s], range(1))
    pass_on(1, right, least)

    def natural(part):
        for row in range(3):
            for yy in range(Y):
                first = row * 64 + yy * 16
                to = pl.ds(pl.multiple_of(part * 48 + yy * ROWS + row * 16, 16), 16)
                for low in range(8):
                    values = right[part, first : first + 16, low * C : low * C + C]
                    residues[low, to, :] = values.astype(F32)

    def permute(low):
        for b in range(3):
            rows = at(low * 4 + b, 32, 32)
            for k in range(8):
                values = residues[k, pl.ds(low + 8 * b, 32, stride=24), :]
                permuted[rows, k * C : k * C + C] = values.astype(BF16)
        permuted[at(low * 4 + 3, 32, 32), :] = jnp.zeros((32, WIDE), BF16)

    def triangle(rows):
        from_matrix(rows, lambda kept, columns: nt(left[s, kept], permuted[columns, :]))
        turn_back(TRI, rows)

    for d in (0, 2):
        s_wait(0, right, mate(d), most)
        s_wait(1, right, mate(d), least)
    loop(S, natural)
    loop(8, permute)
    triangle(range(1))
    z_start_back(T0)
    z_wait(A3)
    turn_up(LEFT, range(1, 3))
    matrix(left.at[s], range(1, 3))
    triangle(range(1, 2))
    z_start_back(T1)
    triangle(last)
    z_start_back(T2)

    def tile(phase, first):
        def body(own):
            block = first + own
            values = jnp.concatenate([yr[phase][k, own] for k in range(G)], axis=0)
            normed, inverse = normalize(values.astype(F32))
            rounded = normed.astype(BF16)
            linear = nn(wt[5 * C :], rounded)
            gate = proj[block, 4 * C :]
            updates[block] = gate * linear
            grad_linear = (upstream[block] * gate).astype(BF16)
            logit = (upstream[block] * linear * gate * (1.0 - gate)).astype(BF16)
            stack[block, 4 * C :] = logit
            gwin[:, 4 * C : 5 * C] += nt(xb[block], logit)
            gwin[:, 5 * C :] += nt(rounded, grad_linear)
            grad_xout = nn(weights_ref[5], grad_linear)
            grad = norm_backward(grad_xout, normed, inverse).astype(BF16)
            for k in range(G):
                ys[phase + G0 - T0][k, own] = grad[k * 16 : k * 16 + 16]

        loop(len(PHASES[phase]), body)

    z_wait(T0)
    y_start_back(T0)
    share(2, left, full)
    y_wait(T0)
    tile(T0, 0)
    y_start(G0)
    z_wait(T1)
    y_start_back(T1)
    y_wait(G0)
    z_start_up(G0)
    z_wait(T2)
    y_start_back(T2)
    y_wait(T1)
    tile(T1, 2)
    y_start(G1)
    y_wait(T2)
    tile(T2, 6)
    y_start(G2)
    y_wait(G1)
    z_start_up(G1)
    y_wait(G2)
    z_start_up(G2)
    early = summing(0, 4)
    early[0]()

    def update_rows(row):
        rows = rows_of([updates[row * 3 + b] for b in range(3)])
        upd_v[at(row, TILE_ROWS, TILE_ROWS), :] = rows.astype(BF16)

    loop(3, update_rows)
    store_upd = pltpu.make_async_copy(upd_v, upd_hbm, local.at[0])
    store_upd.start()
    pass_on(2, left, full)

    def left_gradient(rows):
        turn_up(GRAD, rows)
        matrix(gmat, rows)
        from_matrix(rows, lambda kept, columns: nn(gmat[kept], permuted[:, columns]))
        turn_back(BACK_L, rows)

    def give(which, d):
        src, dst = (gts0, gtr0) if which == 0 else (gts1, gtr1)
        return s_copy(3 + which, src.at[mate(d)], dst.at[s], s, mate(d))

    def columns_of(part):
        gts0[part] = nt(order[part], gmat[:128]).astype(BF16)

    def last_columns_of(part):
        gts1[part, :, :64] = nt(order[part], gmat[128:]).astype(BF16)

    z_wait(G0)
    z_wait(G1)
    left_gradient(two)
    z_start_back(B0)
    loop(S, columns_of)
    loop(S - 1, lambda d: give(0, d).start())
    z_wait(G2)
    left_gradient(last)
    z_start_back(B1)
    loop(S, last_columns_of)
    loop(S - 1, lambda d: give(1, d).start())
    gtr0[s] = gts0[s]
    gtr1[s] = gts1[s]
    early[1]()
    for d in (0, 2):
        s_wait(2, left, mate(d), full)
    loop(S - 1, lambda d: s_wait(3, gtr0, mate(d), full))
    loop(S - 1, lambda d: s_wait(4, gtr1, mate(d), full))

    def join(part):
        gs[part, :, :128] = gtr0[part]
        gs[part, :, 128:ROWS] = gtr1[part, :, :64]

    loop(S, join)
    from_matrix(
        whole,
        lambda kept, columns: sum(nn(gs[k, :, :ROWS], left[k, :, columns]) for k in range(S)),
    )
    turn_back(BACK_R, two)
    z_start_back(B2)
    turn_back(BACK_R, last)
    z_start_back(B3)
    early[2]()

    def grads_of(array, phase, first, block_first, count):
        def body(step):
            block, own = block_first + step, first + step
            values = jnp.concatenate([yr[phase][k, own] for k in range(G)], axis=0)
            grad = values.astype(F32) * mask_ref[block]
            row = 2 * array * C
            value = proj[block, row : row + C]
            gate = jax.nn.sigmoid(proj[block, row + C : row + 2 * C])
            pieces = (grad * gate, grad * value * gate * (1.0 - gate))
            for k in range(2):
                piece = pieces[k].astype(BF16)
                columns = slice(row + k * C, row + (k + 1) * C)
                stack[block, columns] = piece
                gwin[:, columns] += nt(xb[block], piece)

        loop(count, body)

    z_wait(B0)
    y_start_back(B0)
    z_wait(B1)
    y_start_back(B1)
    early[3]()
    y_wait(B0)
    grads_of(0, B0, 0, 0, 6)
    y_wait(B1)
    grads_of(0, B1, 0, 6, 2)
    z_wait(B2)
    y_start_back(B2)
    y_wait(B2)
    grads_of(0, B2, 0, 8, 1)
    middle = summing(1, 0)
    middle[0]()
    grads_of(1, B2, 1, 0, 5)
    z_wait(B3)
    y_start_back(B3)
    early[4]()
    middle[1]()
    y_wait(B3)
    grads_of(1, B3, 0, 5, 4)
    late = summing(2, 2)
    late[0]()
    middle[2]()

    def store_gpair(row):
        rows = at(row, TILE_ROWS, TILE_ROWS)
        return pltpu.make_async_copy(gpair_v.at[rows], gpair_hbm.at[rows], local.at[3 + row])

    def finish(row):
        grads = []
        for b in range(3):
            block = row * 3 + b
            grads.append(norm_backward(nn(wback[...], stack[block]), xn[block], inv[block]))
        gpair_v[at(row, TILE_ROWS, TILE_ROWS), :] = rows_of(grads)
        store_gpair(row).start()

    loop(3, finish)
    late[1]()
    middle[3]()
    late[2]()
    late[3]()
    middle[4]()
    late[4]()

    store_upd.wait()
    loop(3, lambda row: store_gpair(row).wait())
    for phase in range(len(PHASES)):
        loop(G - 1, lambda d, p=phase: y_copy(p, next_g(d), g).wait_send())
        loop(Z - 1, lambda d, p=phase: z_copy(p, next_z(d), z).wait_send())
    for phase, (ref, rows) in enumerate(((right, most), (right, least), (left, full))):
        for d in range(2):
            part = ref.at[s, rows]
            s_copy(phase, part, part, s, mate(d)).wait_send()
        passing_on(phase, ref, rows).wait_send()
    for which in range(2):
        loop(S - 1, lambda d, w=which: give(w, d).wait_send())
    early[5]()
    middle[5]()
    late[5]()


def on_device(pair, pair_mask, weights, cotangent):
    pixels = pair.shape[0] * pair.shape[1]
    mask = pair_mask.astype(F32).reshape(3, 16, 3, 8).transpose(0, 2, 1, 3).reshape(BLOCKS, 1, C)
    vmem = pl.BlockSpec(memory_space=pltpu.VMEM)
    anywhere = pl.BlockSpec(memory_space=pl.ANY)

    def sems(*shape):
        return [pltpu.SemaphoreType.DMA(shape)] * 2

    def sum_buffers():
        one = [pltpu.VMEM((16, C), F32), pltpu.VMEM((G, 16, C), F32)]
        two = [pltpu.VMEM((16, C), F32), pltpu.VMEM((S, 16, C), F32)]
        last = [pltpu.VMEM((16, C), BF16), pltpu.VMEM((Z, 16, C), BF16)]
        return [pltpu.VMEM((Z, 16, C), BF16)] * 2 + one + two + last

    y_buffers = [pltpu.VMEM((G, len(items), 16, C), BF16) for items in PHASES]
    z_buffers = [pltpu.VMEM((Z, rows, C), BF16) for rows in HELD]
    update, grad_pair, grad_weights = pl.pallas_call(
        kernel,
        out_shape=(
            jax.ShapeDtypeStruct((pixels, C), BF16),
            jax.ShapeDtypeStruct((pixels, C), F32),
            jax.ShapeDtypeStruct((6, C, C), F32),
        ),
        in_specs=[anywhere] * 3 + [vmem] * 2,
        out_specs=(anywhere, anywhere, vmem),
        scratch_shapes=[
            pltpu.VMEM((pixels, C), BF16),
            pltpu.VMEM((pixels, C), BF16),
            pltpu.VMEM((S, ROWS, WIDE), BF16),
            pltpu.VMEM((pixels, C), BF16),
            pltpu.VMEM((pixels, C), F32),
            pltpu.VMEM((6 * C, C), BF16),
            pltpu.VMEM((C, 5 * C), BF16),
            pltpu.VMEM((BLOCKS, 5 * C, C), F32),
            pltpu.VMEM((BLOCKS, C, C), F32),
            pltpu.VMEM((BLOCKS, C, C), BF16),
            pltpu.VMEM((BLOCKS, 1, C), F32),
            pltpu.VMEM((BLOCKS, 5 * C, C), BF16),
            pltpu.VMEM((2, BLOCKS, C, C), BF16),
            pltpu.VMEM((Z * max(HELD), C), F32),
            pltpu.VMEM((12 * C, C), F32),
            pltpu.VMEM((S, ROWS, WIDE), BF16),
            pltpu.VMEM((S, ROWS, WIDE), BF16),
            pltpu.VMEM((WIDE, WIDE), BF16),
            pltpu.VMEM((ROWS, WIDE), BF16),
            pltpu.VMEM((8, S * ROWS, C), F32),
            pltpu.VMEM((S, ROWS, 256), BF16),
            *[pltpu.VMEM((S, ROWS, C), BF16)] * 4,
            pltpu.VMEM((C, 6 * C), F32),
            pltpu.VMEM((BLOCKS, C, C), F32),
            pltpu.VMEM((BLOCKS, C, C), F32),
            *y_buffers,
            *y_buffers,
            *z_buffers,
            *z_buffers,
            *[pltpu.VMEM((Z * rows, C), F32) for rows in HELD],
            *[buffer for _ in range(3) for buffer in sum_buffers()],
            *sems(len(PHASES), G),
            *sems(len(PHASES), Z),
            *sems(5, S),
            *[sem for _ in range(3) for n in (Z, G, S, Z) for sem in sems(n)],
            pltpu.SemaphoreType.DMA((6,)),
        ],
        compiler_params=pltpu.CompilerParams(
            collective_id=0, has_side_effects=True, vmem_limit_bytes=56 * 1024 * 1024
        ),
    )(
        pair.reshape(pixels, C),
        cotangent.reshape(pixels, C),
        jnp.asarray(column_order()),
        mask,
        weights,
    )
    return update.reshape(pair.shape), grad_pair.reshape(pair.shape), grad_weights


def solution(mesh):
    placed = (P("row", "col", None), P("row", "col"), P(), P("row", "col", None))
    return jax.shard_map(
        on_device,
        mesh=mesh,
        in_specs=placed,
        out_specs=(P("row", "col", None), P("row", "col", None), P()),
        check_vma=False,
    )
```

```python
import jax
import jax.numpy as jnp
import numpy as np
from jax import lax
from jax.experimental import pallas as pl
from jax.experimental.pallas import tpu as pltpu
from jax.sharding import PartitionSpec as P


F32 = jnp.float32
BF16 = jnp.bfloat16
C = 128
BLOCKS = 9
Y, S, Z, G = 4, 4, 16, 8
ROWS = 192
WIDE = 1024
TILE_ROWS = 384
MESH = pl.DeviceIdType.MESH
RIGHT, LEFT, TRI, GRAD, BACK_L, BACK_R = range(6)
A0, A1, A2, A3, T0, T1, T2, G0, G1, G2, B0, B1, B2, B3 = range(14)


def some(array, first, last):
    return tuple((array, block) for block in range(first, last))


PHASES = (
    some(RIGHT, 0, 6),
    some(RIGHT, 6, 9) + some(LEFT, 0, 1),
    some(LEFT, 1, 3),
    some(LEFT, 3, 9),
    some(TRI, 0, 2),
    some(TRI, 2, 6),
    some(TRI, 6, 9),
    some(GRAD, 0, 2),
    some(GRAD, 2, 6),
    some(GRAD, 6, 9),
    some(BACK_L, 0, 6),
    some(BACK_L, 6, 8),
    some(BACK_L, 8, 9) + some(BACK_R, 0, 5),
    some(BACK_R, 5, 9),
)
WHERE = {item: (phase, k) for phase, items in enumerate(PHASES) for k, item in enumerate(items)}
HELD = tuple((len(items) * 8 + 15) // 16 * 16 for items in PHASES)


def nt(a, b):
    return lax.dot_general(a, b, (((1,), (1,)), ((), ())), preferred_element_type=F32)


def nn(a, b):
    return lax.dot_general(a, b, (((1,), (0,)), ((), ())), preferred_element_type=F32)


def normalize(values):
    average = jnp.mean(values, axis=0, keepdims=True)
    centred = values - average
    variance = jnp.mean(centred * centred, axis=0, keepdims=True)
    inverse = lax.rsqrt(variance + 1e-05)
    return centred * inverse, inverse


def norm_backward(upstream, normed, inverse):
    first = jnp.mean(upstream, axis=0, keepdims=True)
    second = jnp.mean(upstream * normed, axis=0, keepdims=True)
    return inverse * (upstream - first - normed * second)


def column_order():
    low, block, tile = np.meshgrid(np.arange(8), np.arange(3), np.arange(32), indexing="ij")
    residue = (tile * 24 + block * 8 + low).reshape(-1)
    place = (low * 128 + block * 32 + tile).reshape(-1)
    y, s, inner = residue // 192, residue // 48 % 4, residue % 48
    order = np.zeros((S, ROWS, WIDE), np.float32)
    order[s, inner // 16 * 64 + y * 16 + inner % 16, place] = 1
    return order.astype(jnp.bfloat16)


def loop(count, body):
    def step(i, carry):
        body(i)
        return carry

    lax.fori_loop(0, count, step, 0)


def at(start, size, unit=8):
    return pl.ds(pl.multiple_of(start * unit, unit), size)


def kernel(
    pair_hbm,
    cot_hbm,
    order_hbm,
    mask_ref,
    weights_ref,
    upd_hbm,
    gpair_hbm,
    gw_ref,
    pair_v,
    cot_v,
    order,
    upd_v,
    gpair_v,
    wt,
    wback,
    proj,
    xn,
    xb,
    inv,
    stack,
    act,
    picked,
    turned,
    left,
    right,
    permuted,
    gmat,
    residues,
    gs,
    gts0,
    gtr0,
    gts1,
    gtr1,
    gwin,
    upstream,
    updates,
    *rest,
):
    rest = list(rest)
    ys, yr, zs, zr, flats = ([rest.pop(0) for _ in PHASES] for _ in range(5))
    sums = [[rest.pop(0) for _ in range(8)] for _ in range(3)]
    y_send, y_recv, z_send, z_recv, s_send, s_recv = (rest.pop(0) for _ in range(6))
    w_sems = [rest.pop(0) for _ in range(3)]
    local = rest.pop(0)

    r = lax.axis_index("row")
    q = lax.axis_index("col")
    y, s = r // 4, r % 4
    half, z = q // 16, q % 16
    g = y * 2 + half

    def group(other):
        return {"row": (other // 2) * 4 + s, "col": (other % 2) * 16 + z}

    def along(other):
        return {"row": r, "col": half * 16 + other}

    def mate(d):
        return ((s // 2 + (d + 1) // 2) % 2) * 2 + (s % 2 + (d + 1) % 2) % 2

    def shared(other):
        return {"row": y * 4 + other, "col": q}

    def next_g(d):
        return (g + 1 + d) % G

    def next_z(step):
        t = Z - 1 - step
        hop = ((t + 1) // 2) * (2 * (t % 2) - 1)
        return (z + hop + Z) % Z

    barrier = pltpu.get_barrier_semaphore()

    def greet(device):
        pl.semaphore_signal(barrier, inc=1, device_id=device, device_id_type=MESH)

    loop(Z - 1, lambda d: greet(along(next_z(d))))
    loop(G - 1, lambda d: greet(group(next_g(d))))
    loop(S - 1, lambda d: greet(shared(mate(d))))

    load_pair = pltpu.make_async_copy(pair_hbm, pair_v, local.at[0])
    load_cot = pltpu.make_async_copy(cot_hbm, cot_v, local.at[1])
    load_order = pltpu.make_async_copy(order_hbm, order, local.at[2])
    load_pair.start()
    load_cot.start()
    load_order.start()

    def all_of(ref, count, send_sem, recv_sem):
        part = ref.at[pl.ds(0, count)]
        return pltpu.make_async_remote_copy(
            src_ref=part,
            dst_ref=part,
            send_sem=send_sem,
            recv_sem=recv_sem,
            device_id=along(next_z(0)),
            device_id_type=MESH,
        )

    def y_copy(phase, to, slot):
        return pltpu.make_async_remote_copy(
            src_ref=ys[phase].at[to],
            dst_ref=yr[phase].at[slot],
            send_sem=y_send.at[phase],
            recv_sem=y_recv.at[phase],
            device_id=group(to),
            device_id_type=MESH,
        )

    def y_start(phase):
        loop(G - 1, lambda d: y_copy(phase, next_g(d), g).start())
        yr[phase][g] = ys[phase][g]

    def y_all(phase):
        return all_of(yr[phase], G - 1, y_send.at[phase], y_recv.at[phase])

    def y_wait(phase):
        y_all(phase).wait_recv()

    def z_copy(phase, to, slot):
        return pltpu.make_async_remote_copy(
            src_ref=zs[phase].at[to],
            dst_ref=zr[phase].at[slot],
            send_sem=z_send.at[phase],
            recv_sem=z_recv.at[phase],
            device_id=along(to),
            device_id_type=MESH,
        )

    def z_all(phase):
        return all_of(zr[phase], Z - 1, z_send.at[phase], z_recv.at[phase])

    def z_start(phase, make):
        def send(step):
            to = next_z(step)
            zs[phase][to] = make(to)
            z_copy(phase, to, z).start()

        loop(Z - 1, send)
        zr[phase][z] = make(z)

    def z_wait(phase):
        rows = HELD[phase]
        flat = flats[phase]

        def widen(step):
            for k in range(4):
                frm = step * 4 + k
                flat[at(frm * (rows // 16), rows, 16), :] = zr[phase][frm].astype(F32)

        z_all(phase).wait_recv()
        loop(Z // 4, widen)

    def y_fill(phase):
        for k, (array, block) in enumerate(PHASES[phase]):
            for other in range(G):
                ys[phase][other, k] = act[array, block, other * 16 : other * 16 + 16]

    def z_start_up(phase):
        blocks, rows = len(PHASES[phase]), HELD[phase]

        def spread(k):
            for other in range(G):
                picked[at(other * blocks + k, 16, 16), :] = yr[phase][other, k].astype(F32)

        loop(blocks, spread)
        z_start(phase, lambda to: picked[pl.ds(to, rows, stride=Z), :].astype(BF16))

    def z_start_back(phase):
        rows = HELD[phase]
        z_start(phase, lambda to: flats[phase][at(to * (rows // 16), rows, 16), :].astype(BF16))

    def y_start_back(phase):
        blocks, rows = len(PHASES[phase]), HELD[phase]

        def fill(other):
            for k in range(blocks):
                values = flats[phase][pl.ds(other * blocks + k, Z, stride=rows), :]
                ys[phase][other, k] = values.astype(BF16)

        def send(d):
            fill(next_g(d))
            y_copy(phase, next_g(d), g).start()

        loop(G - 1, send)
        fill(g)
        yr[phase][g] = ys[phase][g]

    def place(array, block, part):
        phase, k = WHERE[array, block]
        return flats[phase], pl.ds(part * len(PHASES[phase]) + k, Z, stride=HELD[phase])

    def turn_up(array, rows):
        for row in rows:

            for yy in range(Y):
                pieces = []
                for b in range(3):
                    for hh in range(2):
                        flat, spot = place(array, row * 3 + b, yy * 2 + hh)
                        pieces.append(flat[spot, :])
                pieces.append(jnp.zeros((32, C), F32))
                turned[(row * Y + yy) * C : (row * Y + yy + 1) * C, :] = jnp.concatenate(pieces, axis=0).T

    def turn_back(array, rows):
        for row in rows:

            for yy in range(Y):
                values = turned[(row * Y + yy) * C : (row * Y + yy + 1) * C, :].T
                for b in range(3):
                    for hh in range(2):
                        first = b * 32 + hh * 16
                        flat, spot = place(array, row * 3 + b, yy * 2 + hh)
                        flat[spot, :] = values[first : first + 16]

    def low_columns(low):
        return at(low, C, C)

    def held(rows):
        size = 64 * len(rows)
        return slice(rows[0] * 64, rows[0] * 64 + size), lambda low: pl.ds(
            rows[0] * 512 + low, size, stride=8
        )

    def matrix(ref, rows):
        kept, where = held(rows)

        def body(pair):
            for low in (2 * pair, 2 * pair + 1):
                ref[kept, low_columns(low)] = turned[where(low), :].astype(BF16)

        loop(4, body)

    def from_matrix(rows, make):
        kept, where = held(rows)

        def body(pair):
            values = make(kept, at(pair, 2 * C, 2 * C))
            turned[where(2 * pair), :] = values[:, :C]
            turned[where(2 * pair + 1), :] = values[:, C:]

        loop(4, body)

    def s_copy(phase, src, dst, slot, to):
        return pltpu.make_async_remote_copy(
            src_ref=src,
            dst_ref=dst,
            send_sem=s_send.at[phase, to],
            recv_sem=s_recv.at[phase, slot],
            device_id=shared(to),
            device_id_type=MESH,
        )

    def share(phase, ref, rows):
        part = ref.at[s, rows]
        s_copy(phase, part, part, s, mate(1)).start()
        s_copy(phase, part, part, s, mate(0)).start()

    def passing_on(phase, ref, rows):
        return pltpu.make_async_remote_copy(
            src_ref=ref.at[mate(1), rows],
            dst_ref=ref.at[mate(1), rows],
            send_sem=s_send.at[phase, mate(2)],
            recv_sem=s_recv.at[phase, mate(1)],
            device_id=shared(mate(0)),
            device_id_type=MESH,
        )

    def s_wait(phase, ref, slot, rows):
        part = ref.at[slot, rows]
        s_copy(phase, part, part, slot, slot).wait_recv()

    def pass_on(phase, ref, rows):
        s_wait(phase, ref, mate(1), rows)
        passing_on(phase, ref, rows).start()

    def summing(which, first):
        a_s, a_r, b_s, b_r, c_s, c_r, d_s, d_r = sums[which]
        sems = w_sems[which]

        def copy(step, src, dst, to, slot, device):
            return pltpu.make_async_remote_copy(
                src_ref=src,
                dst_ref=dst,
                send_sem=sems.at[step, 0],
                recv_sem=sems.at[step, 1],
                device_id=device,
                device_id_type=MESH,
            )

        copies = (
            lambda to, slot: copy(0, a_s.at[to], a_r.at[slot], to, slot, along(to)),
            lambda to, slot: copy(1, b_s, b_r.at[slot], to, slot, group(to)),
            lambda to, slot: copy(2, c_s, c_r.at[slot], to, slot, shared(to)),
            lambda to, slot: copy(3, d_s, d_r.at[slot], to, slot, along(to)),
        )
        others = ((Z - 1, next_z), (G - 1, next_g), (S - 1, mate), (Z - 1, next_z))
        mine = (z, g, s, z)

        def start(step):
            count, other = others[step]
            loop(count, lambda d: copies[step](other(d), mine[step]).start())

        def every(step):
            return all_of(
                (a_r, b_r, c_r, d_r)[step], others[step][0], sems.at[step, 0], sems.at[step, 1]
            )

        def wait(step):
            every(step).wait_recv()

        def one():
            for k in range(Z):
                rows, columns = (k % 8) * 16, (first + k // 8) * C
                a_s[k] = gwin[rows : rows + 16, columns : columns + C].astype(BF16)
            start(0)
            a_r[z] = a_s[z]

        def two():
            wait(0)
            b_s[...] = sum(a_r[k].astype(F32) for k in range(Z))
            start(1)
            b_r[g] = b_s[...]

        def three():
            wait(1)
            c_s[...] = sum(b_r[k] for k in range(G))
            start(2)
            c_r[s] = c_s[...]

        def four():
            wait(2)
            d_s[...] = (sum(c_r[k] for k in range(S)) * (1.0 / 768.0)).astype(BF16)
            start(3)
            d_r[z] = d_s[...]

        def five():
            wait(3)
            for k in range(Z):
                gw_ref[first + k // 8, (k % 8) * 16 : (k % 8) * 16 + 16] = d_r[k].astype(F32)

        def sent():
            for step in range(len(others)):
                every(step).wait_send()

        return one, two, three, four, five, sent

    def turn_weight(m):
        wt[m * C : (m + 1) * C] = weights_ref[m].astype(F32).T.astype(BF16)

    for m in (2, 3):
        turn_weight(m)

    def tile_rows(ref, row):
        return ref[at(row, TILE_ROWS, TILE_ROWS), :].astype(F32).reshape(16, 24, C)

    def block_of(values, b):
        return values[:, b * 8 : b * 8 + 8, :].reshape(C, C).T

    def rows_of(blocks):
        return jnp.concatenate([b.T.reshape(16, 8, C) for b in blocks], axis=1).reshape(TILE_ROWS, C)

    load_pair.wait()

    def activate(block, array):
        first = 2 * array * C
        p = nn(wt[first : first + 2 * C], xb[block])
        proj[block, first : first + 2 * C] = p
        value = mask_ref[block] * jax.nn.sigmoid(p[C:]) * p[:C]
        act[RIGHT if array else LEFT, block] = value.astype(BF16)

    def project_right(row):
        values = tile_rows(pair_v, row)
        for b in range(3):
            block = row * 3 + b
            normed, inverse = normalize(block_of(values, b))
            xn[block] = normed
            xb[block] = normed.astype(BF16)
            inv[block] = inverse
            activate(block, 1)

    def project_gate(block):
        proj[block, 4 * C :] = jax.nn.sigmoid(nn(wt[4 * C : 5 * C], xb[block]))

    loop(3, project_right)
    y_fill(A0)
    pl.semaphore_wait(barrier, Z + G + S - 3)

    y_start(A0)
    for m in (0, 1):
        turn_weight(m)
    loop(BLOCKS, lambda block: activate(block, 0))
    y_fill(A1)
    y_start(A1)
    y_fill(A2)
    y_fill(A3)
    y_wait(A0)
    z_start_up(A0)
    y_start(A2)
    y_wait(A1)
    z_start_up(A1)
    y_start(A3)
    y_wait(A2)
    z_start_up(A2)
    y_wait(A3)
    z_start_up(A3)
    for m in (4, 5):
        turn_weight(m)
    loop(BLOCKS, project_gate)
    for m in range(5):
        wback[:, m * C : (m + 1) * C] = weights_ref[m]
    gwin[...] = jnp.zeros_like(gwin)
    load_cot.wait()

    def turn_cotangent(row):
        values = tile_rows(cot_v, row)
        for b in range(3):
            upstream[row * 3 + b] = block_of(values, b)

    loop(3, turn_cotangent)
    load_order.wait()
    whole, two, last = range(3), range(2), range(2, 3)
    most, least, full = slice(0, 128), slice(128, 192), slice(0, 192)
    z_wait(A0)
    turn_up(RIGHT, two)
    matrix(right.at[s], two)
    share(0, right, most)
    z_wait(A1)
    turn_up(RIGHT, last)
    matrix(right.at[s], last)
    share(1, right, least)
    pass_on(0, right, most)
    z_wait(A2)
    turn_up(LEFT, range(1))
    matrix(left.at[s], range(1))
    pass_on(1, right, least)

    def natural(part):
        for row in range(3):
            for yy in range(Y):
                first = row * 64 + yy * 16
                to = pl.ds(pl.multiple_of(part * 48 + yy * ROWS + row * 16, 16), 16)
                for low in range(8):
                    values = right[part, first : first + 16, low * C : low * C + C]
                    residues[low, to, :] = values.astype(F32)

    def permute(low):
        for b in range(3):
            rows = at(low * 4 + b, 32, 32)
            for k in range(8):
                values = residues[k, pl.ds(low + 8 * b, 32, stride=24), :]
                permuted[rows, k * C : k * C + C] = values.astype(BF16)
        permuted[at(low * 4 + 3, 32, 32), :] = jnp.zeros((32, WIDE), BF16)

    def triangle(rows):
        from_matrix(rows, lambda kept, columns: nt(left[s, kept], permuted[columns, :]))
        turn_back(TRI, rows)

    for d in (0, 2):
        s_wait(0, right, mate(d), most)
        s_wait(1, right, mate(d), least)
    loop(S, natural)
    loop(8, permute)
    triangle(range(1))
    z_start_back(T0)
    z_wait(A3)
    turn_up(LEFT, range(1, 3))
    matrix(left.at[s], range(1, 3))
    triangle(range(1, 2))
    z_start_back(T1)
    triangle(last)
    z_start_back(T2)

    def tile(phase, first):
        def body(own):
            block = first + own
            values = jnp.concatenate([yr[phase][k, own] for k in range(G)], axis=0)
            normed, inverse = normalize(values.astype(F32))
            rounded = normed.astype(BF16)
            linear = nn(wt[5 * C :], rounded)
            gate = proj[block, 4 * C :]
            updates[block] = gate * linear
            grad_linear = (upstream[block] * gate).astype(BF16)
            logit = (upstream[block] * linear * gate * (1.0 - gate)).astype(BF16)
            stack[block, 4 * C :] = logit
            gwin[:, 4 * C : 5 * C] += nt(xb[block], logit)
            gwin[:, 5 * C :] += nt(rounded, grad_linear)
            grad_xout = nn(weights_ref[5], grad_linear)
            grad = norm_backward(grad_xout, normed, inverse).astype(BF16)
            for k in range(G):
                ys[phase + G0 - T0][k, own] = grad[k * 16 : k * 16 + 16]

        loop(len(PHASES[phase]), body)

    z_wait(T0)
    y_start_back(T0)
    share(2, left, full)
    y_wait(T0)
    tile(T0, 0)
    y_start(G0)
    z_wait(T1)
    y_start_back(T1)
    y_wait(G0)
    z_start_up(G0)
    z_wait(T2)
    y_start_back(T2)
    y_wait(T1)
    tile(T1, 2)
    y_start(G1)
    y_wait(T2)
    tile(T2, 6)
    y_start(G2)
    y_wait(G1)
    z_start_up(G1)
    y_wait(G2)
    z_start_up(G2)
    early = summing(0, 4)
    early[0]()

    def update_rows(row):
        rows = rows_of([updates[row * 3 + b] for b in range(3)])
        upd_v[at(row, TILE_ROWS, TILE_ROWS), :] = rows.astype(BF16)

    loop(3, update_rows)
    store_upd = pltpu.make_async_copy(upd_v, upd_hbm, local.at[0])
    store_upd.start()
    pass_on(2, left, full)

    def left_gradient(rows):
        from_matrix(rows, lambda kept, columns: nn(gmat[kept], permuted[:, columns]))
        turn_back(BACK_L, rows)

    def give(which, d):
        src, dst = (gts0, gtr0) if which == 0 else (gts1, gtr1)
        return s_copy(3 + which, src.at[mate(d)], dst.at[s], s, mate(d))

    def columns_of(part):
        gts0[part] = nt(order[part], gmat[:128]).astype(BF16)

    def last_columns_of(part):
        gts1[part, :, :64] = nt(order[part], gmat[128:]).astype(BF16)

    z_wait(G0)
    z_wait(G1)
    turn_up(GRAD, two)
    matrix(gmat, two)
    left_gradient(two)
    z_start_back(B0)
    loop(S, columns_of)
    loop(S - 1, lambda d: give(0, d).start())
    z_wait(G2)
    turn_up(GRAD, last)
    matrix(gmat, last)
    loop(S, last_columns_of)
    loop(S - 1, lambda d: give(1, d).start())
    left_gradient(last)
    z_start_back(B1)
    gtr0[s] = gts0[s]
    gtr1[s] = gts1[s]
    early[1]()
    for d in (0, 2):
        s_wait(2, left, mate(d), full)
    loop(S - 1, lambda d: s_wait(3, gtr0, mate(d), full))
    loop(S - 1, lambda d: s_wait(4, gtr1, mate(d), full))

    def join(part):
        gs[part, :, :128] = gtr0[part]
        gs[part, :, 128:ROWS] = gtr1[part, :, :64]

    loop(S, join)
    from_matrix(
        whole,
        lambda kept, columns: sum(nn(gs[k, :, :ROWS], left[k, :, columns]) for k in range(S)),
    )
    turn_back(BACK_R, two)
    z_start_back(B2)
    turn_back(BACK_R, last)
    z_start_back(B3)
    early[2]()

    def grads_of(array, phase, first, block_first, count):
        def body(step):
            block, own = block_first + step, first + step
            values = jnp.concatenate([yr[phase][k, own] for k in range(G)], axis=0)
            grad = values.astype(F32) * mask_ref[block]
            row = 2 * array * C
            value = proj[block, row : row + C]
            gate = jax.nn.sigmoid(proj[block, row + C : row + 2 * C])
            pieces = (grad * gate, grad * value * gate * (1.0 - gate))
            for k in range(2):
                piece = pieces[k].astype(BF16)
                columns = slice(row + k * C, row + (k + 1) * C)
                stack[block, columns] = piece
                gwin[:, columns] += nt(xb[block], piece)

        loop(count, body)

    z_wait(B0)
    y_start_back(B0)
    z_wait(B1)
    y_start_back(B1)
    early[3]()
    y_wait(B0)
    grads_of(0, B0, 0, 0, 6)
    y_wait(B1)
    grads_of(0, B1, 0, 6, 2)
    z_wait(B2)
    y_start_back(B2)
    y_wait(B2)
    grads_of(0, B2, 0, 8, 1)
    middle = summing(1, 0)
    middle[0]()
    grads_of(1, B2, 1, 0, 5)
    z_wait(B3)
    y_start_back(B3)
    early[4]()
    middle[1]()
    y_wait(B3)
    grads_of(1, B3, 0, 5, 4)
    late = summing(2, 2)
    late[0]()
    middle[2]()

    def store_gpair(row):
        rows = at(row, TILE_ROWS, TILE_ROWS)
        return pltpu.make_async_copy(gpair_v.at[rows], gpair_hbm.at[rows], local.at[3 + row])

    def finish(row):
        grads = []
        for b in range(3):
            block = row * 3 + b
            grads.append(norm_backward(nn(wback[...], stack[block]), xn[block], inv[block]))
        gpair_v[at(row, TILE_ROWS, TILE_ROWS), :] = rows_of(grads)
        store_gpair(row).start()

    loop(3, finish)
    late[1]()
    middle[3]()
    late[2]()
    late[3]()
    middle[4]()
    late[4]()

    store_upd.wait()
    loop(3, lambda row: store_gpair(row).wait())
    for phase in range(len(PHASES)):
        y_all(phase).wait_send()
        z_all(phase).wait_send()
    for phase, (ref, rows) in enumerate(((right, most), (right, least), (left, full))):
        for d in range(2):
            part = ref.at[s, rows]
            s_copy(phase, part, part, s, mate(d)).wait_send()
        passing_on(phase, ref, rows).wait_send()
    for which in range(2):
        loop(S - 1, lambda d, w=which: give(w, d).wait_send())
    early[5]()
    middle[5]()
    late[5]()


def hand_over(a, b, c, a_out, b_out, c_out, a_v, b_v, c_v, sems):
    held = (a_v, b_v, c_v)
    ins = [pltpu.make_async_copy(x, v, sems.at[k]) for k, (x, v) in enumerate(zip((a, b, c), held))]
    outs = [
        pltpu.make_async_copy(v, x, sems.at[3 + k])
        for k, (x, v) in enumerate(zip((a_out, b_out, c_out), held))
    ]
    for copy in ins:
        copy.start()
    for k in range(3):
        ins[k].wait()
        outs[k].start()
    for copy in outs:
        copy.wait()


def on_device(pair, pair_mask, weights, cotangent):
    pixels = pair.shape[0] * pair.shape[1]
    mask = pair_mask.astype(F32).reshape(3, 16, 3, 8).transpose(0, 2, 1, 3).reshape(BLOCKS, 1, C)
    vmem = pl.BlockSpec(memory_space=pltpu.VMEM)
    anywhere = pl.BlockSpec(memory_space=pl.ANY)

    def sems(*shape):
        return [pltpu.SemaphoreType.DMA(shape)] * 2

    def sum_buffers():
        one = [pltpu.VMEM((16, C), F32), pltpu.VMEM((G, 16, C), F32)]
        two = [pltpu.VMEM((16, C), F32), pltpu.VMEM((S, 16, C), F32)]
        last = [pltpu.VMEM((16, C), BF16), pltpu.VMEM((Z, 16, C), BF16)]
        return [pltpu.VMEM((Z, 16, C), BF16)] * 2 + one + two + last

    y_buffers = [pltpu.VMEM((G, len(items), 16, C), BF16) for items in PHASES]
    z_buffers = [pltpu.VMEM((Z, rows, C), BF16) for rows in HELD]
    update, grad_pair, grad_weights = pl.pallas_call(
        kernel,
        out_shape=(
            jax.ShapeDtypeStruct((pixels, C), BF16),
            jax.ShapeDtypeStruct((pixels, C), F32),
            jax.ShapeDtypeStruct((6, C, C), F32),
        ),
        in_specs=[anywhere] * 3 + [vmem] * 2,
        out_specs=(anywhere, anywhere, vmem),
        scratch_shapes=[
            pltpu.VMEM((pixels, C), BF16),
            pltpu.VMEM((pixels, C), BF16),
            pltpu.VMEM((S, ROWS, WIDE), BF16),
            pltpu.VMEM((pixels, C), BF16),
            pltpu.VMEM((pixels, C), F32),
            pltpu.VMEM((6 * C, C), BF16),
            pltpu.VMEM((C, 5 * C), BF16),
            pltpu.VMEM((BLOCKS, 5 * C, C), F32),
            pltpu.VMEM((BLOCKS, C, C), F32),
            pltpu.VMEM((BLOCKS, C, C), BF16),
            pltpu.VMEM((BLOCKS, 1, C), F32),
            pltpu.VMEM((BLOCKS, 5 * C, C), BF16),
            pltpu.VMEM((2, BLOCKS, C, C), BF16),
            pltpu.VMEM((Z * max(HELD), C), F32),
            pltpu.VMEM((12 * C, C), F32),
            pltpu.VMEM((S, ROWS, WIDE), BF16),
            pltpu.VMEM((S, ROWS, WIDE), BF16),
            pltpu.VMEM((WIDE, WIDE), BF16),
            pltpu.VMEM((ROWS, WIDE), BF16),
            pltpu.VMEM((8, S * ROWS, C), F32),
            pltpu.VMEM((S, ROWS, 256), BF16),
            *[pltpu.VMEM((S, ROWS, C), BF16)] * 4,
            pltpu.VMEM((C, 6 * C), F32),
            pltpu.VMEM((BLOCKS, C, C), F32),
            pltpu.VMEM((BLOCKS, C, C), F32),
            *y_buffers,
            *y_buffers,
            *z_buffers,
            *z_buffers,
            *[pltpu.VMEM((Z * rows, C), F32) for rows in HELD],
            *[buffer for _ in range(3) for buffer in sum_buffers()],
            *sems(len(PHASES)),
            *sems(len(PHASES)),
            *sems(5, S),
            *[pltpu.SemaphoreType.DMA((4, 2))] * 3,
            pltpu.SemaphoreType.DMA((6,)),
        ],
        compiler_params=pltpu.CompilerParams(
            collective_id=0, has_side_effects=True, vmem_limit_bytes=56 * 1024 * 1024
        ),
    )(
        pair.reshape(pixels, C),
        cotangent.reshape(pixels, C),
        jnp.asarray(column_order()),
        mask,
        weights,
    )
    results = (update, grad_pair, grad_weights)
    update, grad_pair, grad_weights = pl.pallas_call(
        hand_over,
        out_shape=tuple(jax.ShapeDtypeStruct(a.shape, a.dtype) for a in results),
        in_specs=[anywhere] * 3,
        out_specs=(anywhere,) * 3,
        scratch_shapes=[
            *[pltpu.VMEM(a.shape, a.dtype) for a in results],
            pltpu.SemaphoreType.DMA((6,)),
        ],
    )(*results)
    return update.reshape(pair.shape), grad_pair.reshape(pair.shape), grad_weights


def solution(mesh):
    placed = (P("row", "col", None), P("row", "col"), P(), P("row", "col", None))
    return jax.shard_map(
        on_device,
        mesh=mesh,
        in_specs=placed,
        out_specs=(P("row", "col", None), P("row", "col", None), P()),
        check_vma=False,
    )
```

```python
import jax
import jax.numpy as jnp
import numpy as np
from jax import lax
from jax.experimental import pallas as pl
from jax.experimental.pallas import tpu as pltpu
from jax.sharding import PartitionSpec as P


F32 = jnp.float32
BF16 = jnp.bfloat16
C = 128
BLOCKS = 9
Y, S, Z, G, W = 4, 4, 16, 8, 32
ROWS = 192
WIDE = 1024
TILE_ROWS = 384
MESH = pl.DeviceIdType.MESH
RIGHT, LEFT, TRI, GRAD, BACK_L, BACK_R = range(6)
A0, A1, A2, A3, A4, T0, T1, T2, G0, G1, G2, B0, B1, B2, B3 = range(15)


def some(array, first, last):
    return tuple((array, block) for block in range(first, last))


PHASES = (
    some(RIGHT, 0, 6),
    some(RIGHT, 6, 9) + some(LEFT, 0, 1),
    some(LEFT, 1, 3),
    some(LEFT, 3, 7),
    some(LEFT, 7, 9),
    some(TRI, 0, 2),
    some(TRI, 2, 6),
    some(TRI, 6, 9),
    some(GRAD, 0, 2),
    some(GRAD, 2, 6),
    some(GRAD, 6, 9),
    some(BACK_L, 0, 6),
    some(BACK_L, 6, 8),
    some(BACK_L, 8, 9) + some(BACK_R, 0, 5),
    some(BACK_R, 5, 9),
)
WHERE = {item: (phase, k) for phase, items in enumerate(PHASES) for k, item in enumerate(items)}
HELD = tuple((len(items) * 8 + 15) // 16 * 16 for items in PHASES)


def nt(a, b):
    return lax.dot_general(a, b, (((1,), (1,)), ((), ())), preferred_element_type=F32)


def nn(a, b):
    return lax.dot_general(a, b, (((1,), (0,)), ((), ())), preferred_element_type=F32)


def normalize(values):
    average = jnp.mean(values, axis=0, keepdims=True)
    centred = values - average
    variance = jnp.mean(centred * centred, axis=0, keepdims=True)
    inverse = lax.rsqrt(variance + 1e-05)
    return centred * inverse, inverse


def norm_backward(upstream, normed, inverse):
    first = jnp.mean(upstream, axis=0, keepdims=True)
    second = jnp.mean(upstream * normed, axis=0, keepdims=True)
    return inverse * (upstream - first - normed * second)


def column_order():
    low, block, tile = np.meshgrid(np.arange(8), np.arange(3), np.arange(32), indexing="ij")
    residue = (tile * 24 + block * 8 + low).reshape(-1)
    place = (low * 128 + block * 32 + tile).reshape(-1)
    y, s, inner = residue // 192, residue // 48 % 4, residue % 48
    order = np.zeros((S, ROWS, WIDE), np.float32)
    order[s, inner // 16 * 64 + y * 16 + inner % 16, place] = 1
    return order.astype(jnp.bfloat16)


def loop(count, body):
    if count <= 9:
        for i in range(count):
            body(i)
        return

    def step(i, carry):
        body(i)
        return carry

    lax.fori_loop(0, count, step, 0)


def at(start, size, unit=8):
    return pl.ds(pl.multiple_of(start * unit, unit), size)


def kernel(
    pair_hbm,
    cot_hbm,
    order_hbm,
    mask_ref,
    weights_ref,
    upd_hbm,
    gpair_hbm,
    gw_ref,
    pair_v,
    cot_v,
    order,
    upd_v,
    gpair_v,
    wt,
    wback,
    proj,
    xn,
    xb,
    inv,
    stack,
    act,
    picked,
    turned,
    left,
    right,
    permuted,
    gmat,
    residues,
    gs,
    gts0,
    gtr0,
    gts1,
    gtr1,
    gwin,
    upstream,
    updates,
    *rest,
):
    rest = list(rest)
    ys, yr, zs, zr, flats = ([rest.pop(0) for _ in PHASES] for _ in range(5))
    sums = [[rest.pop(0) for _ in range(6)] for _ in range(3)]
    y_send, y_recv, z_send, z_recv, s_send, s_recv = (rest.pop(0) for _ in range(6))
    w_sems = [rest.pop(0) for _ in range(3)]
    local = rest.pop(0)

    r = lax.axis_index("row")
    q = lax.axis_index("col")
    y, s = r // 4, r % 4
    half, z = q // 16, q % 16
    g = y * 2 + half
    w = g * S + s

    def group(other):
        return {"row": (other // 2) * 4 + s, "col": (other % 2) * 16 + z}

    def along(other):
        return {"row": r, "col": half * 16 + other}

    def mate(d):
        return ((s // 2 + (d + 1) // 2) % 2) * 2 + (s % 2 + (d + 1) % 2) % 2

    def shared(other):
        return {"row": y * 4 + other, "col": q}

    def next_g(d):
        return (g + 1 + d) % G

    def across(other):
        return {"row": (other // 8) * 4 + other % 4, "col": (other // 4 % 2) * 16 + z}

    def next_w(d):
        return (w + 1 + d) % W

    def next_z(step):
        t = Z - 1 - step
        hop = ((t + 1) // 2) * (2 * (t % 2) - 1)
        return (z + hop + Z) % Z

    barrier = pltpu.get_barrier_semaphore()

    def greet(device):
        pl.semaphore_signal(barrier, inc=1, device_id=device, device_id_type=MESH)

    loop(Z - 1, lambda d: greet(along(next_z(d))))
    loop(W - 1, lambda d: greet(across(next_w(d))))

    load_pair = pltpu.make_async_copy(pair_hbm, pair_v, local.at[0])
    load_cot = pltpu.make_async_copy(cot_hbm, cot_v, local.at[1])
    load_order = pltpu.make_async_copy(order_hbm, order, local.at[2])
    load_pair.start()
    load_cot.start()
    load_order.start()

    def all_of(ref, count, send_sem, recv_sem):
        part = ref.at[pl.ds(0, count)]
        return pltpu.make_async_remote_copy(
            src_ref=part,
            dst_ref=part,
            send_sem=send_sem,
            recv_sem=recv_sem,
            device_id=along(next_z(0)),
            device_id_type=MESH,
        )

    def y_copy(phase, to, slot):
        return pltpu.make_async_remote_copy(
            src_ref=ys[phase].at[to],
            dst_ref=yr[phase].at[slot],
            send_sem=y_send.at[phase],
            recv_sem=y_recv.at[phase],
            device_id=group(to),
            device_id_type=MESH,
        )

    def y_start(phase):
        loop(G - 1, lambda d: y_copy(phase, next_g(d), g).start())
        yr[phase][g] = ys[phase][g]

    def y_all(phase):
        return all_of(yr[phase], G - 1, y_send.at[phase], y_recv.at[phase])

    def y_wait(phase):
        y_all(phase).wait_recv()

    def z_copy(phase, to, slot):
        return pltpu.make_async_remote_copy(
            src_ref=zs[phase].at[to],
            dst_ref=zr[phase].at[slot],
            send_sem=z_send.at[phase],
            recv_sem=z_recv.at[phase],
            device_id=along(to),
            device_id_type=MESH,
        )

    def z_all(phase):
        return all_of(zr[phase], Z - 1, z_send.at[phase], z_recv.at[phase])

    def z_start(phase, make):
        def send(step):
            to = next_z(step)
            zs[phase][to] = make(to)
            z_copy(phase, to, z).start()

        loop(Z - 1, send)
        zr[phase][z] = make(z)

    def z_wait(phase):
        rows = HELD[phase]
        flat = flats[phase]

        def widen(step):
            for k in range(4):
                frm = step * 4 + k
                flat[at(frm * (rows // 16), rows, 16), :] = zr[phase][frm].astype(F32)

        z_all(phase).wait_recv()
        loop(Z // 4, widen)

    def y_fill(phase):
        for k, (array, block) in enumerate(PHASES[phase]):
            for other in range(G):
                ys[phase][other, k] = act[array, block, other * 16 : other * 16 + 16]

    def z_start_up(phase):
        blocks, rows = len(PHASES[phase]), HELD[phase]

        def spread(k):
            for other in range(G):
                picked[at(other * blocks + k, 16, 16), :] = yr[phase][other, k].astype(F32)

        loop(blocks, spread)
        z_start(phase, lambda to: picked[pl.ds(to, rows, stride=Z), :].astype(BF16))

    def z_start_back(phase):
        rows = HELD[phase]
        z_start(phase, lambda to: flats[phase][at(to * (rows // 16), rows, 16), :].astype(BF16))

    def y_start_back(phase):
        blocks, rows = len(PHASES[phase]), HELD[phase]

        def fill(other):
            for k in range(blocks):
                values = flats[phase][pl.ds(other * blocks + k, Z, stride=rows), :]
                ys[phase][other, k] = values.astype(BF16)

        def send(d):
            fill(next_g(d))
            y_copy(phase, next_g(d), g).start()

        loop(G - 1, send)
        fill(g)
        yr[phase][g] = ys[phase][g]

    def place(array, block, part):
        phase, k = WHERE[array, block]
        return flats[phase], pl.ds(part * len(PHASES[phase]) + k, Z, stride=HELD[phase])

    def turn_up(array, rows):
        for row in rows:

            for yy in range(Y):
                pieces = []
                for b in range(3):
                    for hh in range(2):
                        flat, spot = place(array, row * 3 + b, yy * 2 + hh)
                        pieces.append(flat[spot, :])
                pieces.append(jnp.zeros((32, C), F32))
                turned[(row * Y + yy) * C : (row * Y + yy + 1) * C, :] = jnp.concatenate(pieces, axis=0).T

    def turn_back(array, rows):
        for row in rows:

            for yy in range(Y):
                values = turned[(row * Y + yy) * C : (row * Y + yy + 1) * C, :].T
                for b in range(3):
                    for hh in range(2):
                        first = b * 32 + hh * 16
                        flat, spot = place(array, row * 3 + b, yy * 2 + hh)
                        flat[spot, :] = values[first : first + 16]

    def low_columns(low):
        return at(low, C, C)

    def held(rows):
        size = 64 * len(rows)
        return slice(rows[0] * 64, rows[0] * 64 + size), lambda low: pl.ds(
            rows[0] * 512 + low, size, stride=8
        )

    def matrix(ref, rows):
        kept, where = held(rows)

        def body(pair):
            for low in (2 * pair, 2 * pair + 1):
                ref[kept, low_columns(low)] = turned[where(low), :].astype(BF16)

        loop(4, body)

    def from_matrix(rows, make):
        kept, where = held(rows)

        def body(pair):
            values = make(kept, at(pair, 2 * C, 2 * C))
            turned[where(2 * pair), :] = values[:, :C]
            turned[where(2 * pair + 1), :] = values[:, C:]

        loop(4, body)

    def s_copy(phase, src, dst, slot, to):
        return pltpu.make_async_remote_copy(
            src_ref=src,
            dst_ref=dst,
            send_sem=s_send.at[phase, to],
            recv_sem=s_recv.at[phase, slot],
            device_id=shared(to),
            device_id_type=MESH,
        )

    def share(phase, ref, rows):
        part = ref.at[s, rows]
        s_copy(phase, part, part, s, mate(1)).start()
        s_copy(phase, part, part, s, mate(0)).start()

    def passing_on(phase, ref, rows):
        return pltpu.make_async_remote_copy(
            src_ref=ref.at[mate(1), rows],
            dst_ref=ref.at[mate(1), rows],
            send_sem=s_send.at[phase, mate(2)],
            recv_sem=s_recv.at[phase, mate(1)],
            device_id=shared(mate(0)),
            device_id_type=MESH,
        )

    def s_wait(phase, ref, slot, rows):
        part = ref.at[slot, rows]
        s_copy(phase, part, part, slot, slot).wait_recv()

    def pass_on(phase, ref, rows):
        s_wait(phase, ref, mate(1), rows)
        passing_on(phase, ref, rows).start()

    def summing(which, first):
        a_s, a_r, b_s, b_r, c_s, c_r = sums[which]
        sems = w_sems[which]

        def copy(step, src, dst, to, slot, device):
            return pltpu.make_async_remote_copy(
                src_ref=src,
                dst_ref=dst,
                send_sem=sems.at[step, 0],
                recv_sem=sems.at[step, 1],
                device_id=device,
                device_id_type=MESH,
            )

        copies = (
            lambda to, slot: copy(0, a_s.at[to], a_r.at[slot], to, slot, across(to)),
            lambda to, slot: copy(1, b_s, b_r.at[slot], to, slot, along(to)),
            lambda to, slot: copy(2, c_s, c_r.at[slot], to, slot, across(to)),
        )
        others = ((W - 1, next_w), (Z - 1, next_z), (W - 1, next_w))
        mine = (w, z, w)

        def start(step):
            count, other = others[step]
            loop(count, lambda d: copies[step](other(d), mine[step]).start())

        def every(step):
            return all_of(
                (a_r, b_r, c_r)[step], others[step][0], sems.at[step, 0], sems.at[step, 1]
            )

        def wait(step):
            every(step).wait_recv()

        def one():
            for k in range(W):
                rows, columns = (k % 16) * 8, (first + k // 16) * C
                a_s[k] = gwin[rows : rows + 8, columns : columns + C]
            start(0)
            a_r[w] = a_s[w]

        def two():
            wait(0)
            b_s[...] = sum(a_r[k] for k in range(W))
            start(1)
            b_r[z] = b_s[...]

        def three():
            wait(1)
            c_s[...] = sum(b_r[k] for k in range(Z)) * (1.0 / 768.0)
            start(2)
            c_r[w] = c_s[...]

        def four():
            wait(2)
            for k in range(W):
                gw_ref[first + k // 16, (k % 16) * 8 : (k % 16) * 8 + 8] = c_r[k]

        def sent():
            for step in range(len(others)):
                every(step).wait_send()

        return one, two, three, four, sent

    def turn_weight(m):
        wt[m * C : (m + 1) * C] = weights_ref[m].astype(F32).T.astype(BF16)

    for m in (2, 3):
        turn_weight(m)

    def tile_rows(ref, row):
        return ref[at(row, TILE_ROWS, TILE_ROWS), :].astype(F32).reshape(16, 24, C)

    def block_of(values, b):
        return values[:, b * 8 : b * 8 + 8, :].reshape(C, C).T

    def rows_of(blocks):
        return jnp.concatenate([b.T.reshape(16, 8, C) for b in blocks], axis=1).reshape(TILE_ROWS, C)

    load_pair.wait()

    def activate(block, array):
        first = 2 * array * C
        p = nn(wt[first : first + 2 * C], xb[block])
        proj[block, first : first + 2 * C] = p
        value = mask_ref[block] * jax.nn.sigmoid(p[C:]) * p[:C]
        act[RIGHT if array else LEFT, block] = value.astype(BF16)

    def project_right(row):
        values = tile_rows(pair_v, row)
        for b in range(3):
            block = row * 3 + b
            normed, inverse = normalize(block_of(values, b))
            xn[block] = normed
            xb[block] = normed.astype(BF16)
            inv[block] = inverse
            activate(block, 1)

    def project_gate(block):
        proj[block, 4 * C :] = jax.nn.sigmoid(nn(wt[4 * C : 5 * C], xb[block]))

    loop(3, project_right)
    y_fill(A0)
    pl.semaphore_wait(barrier, Z + W - 2)

    y_start(A0)
    for m in (0, 1):
        turn_weight(m)
    loop(BLOCKS, lambda block: activate(block, 0))
    y_fill(A1)
    y_start(A1)
    y_fill(A2)
    y_fill(A3)
    y_fill(A4)
    y_wait(A0)
    z_start_up(A0)
    y_start(A2)
    y_wait(A1)
    z_start_up(A1)
    y_start(A3)
    y_start(A4)
    y_wait(A2)
    z_start_up(A2)
    y_wait(A3)
    z_start_up(A3)
    y_wait(A4)
    z_start_up(A4)
    for m in (4, 5):
        turn_weight(m)
    loop(BLOCKS, project_gate)
    for m in range(5):
        wback[:, m * C : (m + 1) * C] = weights_ref[m]
    gwin[...] = jnp.zeros_like(gwin)
    load_cot.wait()

    def turn_cotangent(row):
        values = tile_rows(cot_v, row)
        for b in range(3):
            upstream[row * 3 + b] = block_of(values, b)

    loop(3, turn_cotangent)
    load_order.wait()
    whole, two, last = range(3), range(2), range(2, 3)
    most, least, full = slice(0, 128), slice(128, 192), slice(0, 192)
    z_wait(A0)
    turn_up(RIGHT, two)
    matrix(right.at[s], two)
    share(0, right, most)
    z_wait(A1)
    turn_up(RIGHT, last)
    matrix(right.at[s], last)
    share(1, right, least)
    pass_on(0, right, most)
    z_wait(A2)
    turn_up(LEFT, range(1))
    matrix(left.at[s], range(1))
    pass_on(1, right, least)

    def natural(part):
        for row in range(3):
            for yy in range(Y):
                first = row * 64 + yy * 16
                to = pl.ds(pl.multiple_of(part * 48 + yy * ROWS + row * 16, 16), 16)
                for low in range(8):
                    values = right[part, first : first + 16, low * C : low * C + C]
                    residues[low, to, :] = values.astype(F32)

    def permute(low):
        for b in range(3):
            rows = at(low * 4 + b, 32, 32)
            for k in range(8):
                values = residues[k, pl.ds(low + 8 * b, 32, stride=24), :]
                permuted[rows, k * C : k * C + C] = values.astype(BF16)
        permuted[at(low * 4 + 3, 32, 32), :] = jnp.zeros((32, WIDE), BF16)

    def triangle(rows):
        from_matrix(rows, lambda kept, columns: nt(left[s, kept], permuted[columns, :]))
        turn_back(TRI, rows)

    for d in (0, 2):
        s_wait(0, right, mate(d), most)
        s_wait(1, right, mate(d), least)
    loop(S, natural)
    loop(8, permute)
    triangle(range(1))
    z_start_back(T0)
    z_wait(A3)
    turn_up(LEFT, range(1, 2))
    matrix(left.at[s], range(1, 2))
    triangle(range(1, 2))
    z_start_back(T1)
    z_wait(A4)
    turn_up(LEFT, last)
    matrix(left.at[s], last)
    triangle(last)
    z_start_back(T2)

    def tile(phase, first):
        def body(own):
            block = first + own
            values = jnp.concatenate([yr[phase][k, own] for k in range(G)], axis=0)
            normed, inverse = normalize(values.astype(F32))
            rounded = normed.astype(BF16)
            linear = nn(wt[5 * C :], rounded)
            gate = proj[block, 4 * C :]
            updates[block] = gate * linear
            grad_linear = (upstream[block] * gate).astype(BF16)
            logit = (upstream[block] * linear * gate * (1.0 - gate)).astype(BF16)
            stack[block, 4 * C :] = logit
            gwin[:, 4 * C : 5 * C] += nt(xb[block], logit)
            gwin[:, 5 * C :] += nt(rounded, grad_linear)
            grad_xout = nn(weights_ref[5], grad_linear)
            grad = norm_backward(grad_xout, normed, inverse).astype(BF16)
            for k in range(G):
                ys[phase + G0 - T0][k, own] = grad[k * 16 : k * 16 + 16]

        loop(len(PHASES[phase]), body)

    z_wait(T0)
    y_start_back(T0)
    share(2, left, full)
    y_wait(T0)
    tile(T0, 0)
    y_start(G0)
    z_wait(T1)
    y_start_back(T1)
    y_wait(G0)
    z_start_up(G0)
    z_wait(T2)
    y_start_back(T2)
    y_wait(T1)
    tile(T1, 2)
    y_start(G1)
    y_wait(T2)
    tile(T2, 6)
    y_start(G2)
    y_wait(G1)
    z_start_up(G1)
    y_wait(G2)
    z_start_up(G2)
    early = summing(0, 4)
    early[0]()

    def update_rows(row):
        rows = rows_of([updates[row * 3 + b] for b in range(3)])
        upd_v[at(row, TILE_ROWS, TILE_ROWS), :] = rows.astype(BF16)

    loop(3, update_rows)
    store_upd = pltpu.make_async_copy(upd_v, upd_hbm, local.at[0])
    store_upd.start()
    pass_on(2, left, full)

    def left_gradient(rows):
        from_matrix(rows, lambda kept, columns: nn(gmat[kept], permuted[:, columns]))
        turn_back(BACK_L, rows)

    def give(which, d):
        src, dst = (gts0, gtr0) if which == 0 else (gts1, gtr1)
        return s_copy(3 + which, src.at[mate(d)], dst.at[s], s, mate(d))

    def columns_of(part):
        gts0[part] = nt(order[part], gmat[:128]).astype(BF16)

    def last_columns_of(part):
        gts1[part, :, :64] = nt(order[part], gmat[128:]).astype(BF16)

    z_wait(G0)
    z_wait(G1)
    turn_up(GRAD, two)
    matrix(gmat, two)
    left_gradient(two)
    z_start_back(B0)
    loop(S, columns_of)
    loop(S - 1, lambda d: give(0, d).start())
    z_wait(G2)
    turn_up(GRAD, last)
    matrix(gmat, last)
    loop(S, last_columns_of)
    loop(S - 1, lambda d: give(1, d).start())
    left_gradient(last)
    z_start_back(B1)
    gtr0[s] = gts0[s]
    gtr1[s] = gts1[s]
    early[1]()
    for d in (0, 2):
        s_wait(2, left, mate(d), full)
    loop(S - 1, lambda d: s_wait(3, gtr0, mate(d), full))
    loop(S - 1, lambda d: s_wait(4, gtr1, mate(d), full))

    def join(part):
        gs[part, :, :128] = gtr0[part]
        gs[part, :, 128:ROWS] = gtr1[part, :, :64]

    loop(S, join)
    from_matrix(
        whole,
        lambda kept, columns: sum(nn(gs[k, :, :ROWS], left[k, :, columns]) for k in range(S)),
    )
    turn_back(BACK_R, two)
    z_start_back(B2)
    turn_back(BACK_R, last)
    z_start_back(B3)
    early[2]()

    def grads_of(array, phase, first, block_first, count):
        def body(step):
            block, own = block_first + step, first + step
            values = jnp.concatenate([yr[phase][k, own] for k in range(G)], axis=0)
            grad = values.astype(F32) * mask_ref[block]
            row = 2 * array * C
            value = proj[block, row : row + C]
            gate = jax.nn.sigmoid(proj[block, row + C : row + 2 * C])
            pieces = (grad * gate, grad * value * gate * (1.0 - gate))
            for k in range(2):
                piece = pieces[k].astype(BF16)
                columns = slice(row + k * C, row + (k + 1) * C)
                stack[block, columns] = piece
                gwin[:, columns] += nt(xb[block], piece)

        loop(count, body)

    z_wait(B0)
    y_start_back(B0)
    z_wait(B1)
    y_start_back(B1)
    early[3]()
    y_wait(B0)
    grads_of(0, B0, 0, 0, 6)
    y_wait(B1)
    grads_of(0, B1, 0, 6, 2)
    z_wait(B2)
    y_start_back(B2)
    y_wait(B2)
    grads_of(0, B2, 0, 8, 1)
    middle = summing(1, 0)
    middle[0]()
    grads_of(1, B2, 1, 0, 5)
    z_wait(B3)
    y_start_back(B3)
    middle[1]()
    y_wait(B3)
    grads_of(1, B3, 0, 5, 4)
    late = summing(2, 2)
    late[0]()
    middle[2]()

    def store_gpair(row):
        rows = at(row, TILE_ROWS, TILE_ROWS)
        return pltpu.make_async_copy(gpair_v.at[rows], gpair_hbm.at[rows], local.at[3 + row])

    def finish(row):
        grads = []
        for b in range(3):
            block = row * 3 + b
            grads.append(norm_backward(nn(wback[...], stack[block]), xn[block], inv[block]))
        gpair_v[at(row, TILE_ROWS, TILE_ROWS), :] = rows_of(grads)
        store_gpair(row).start()

    loop(3, finish)
    late[1]()
    middle[3]()
    late[2]()
    late[3]()

    store_upd.wait()
    loop(3, lambda row: store_gpair(row).wait())
    for phase in range(len(PHASES)):
        y_all(phase).wait_send()
        z_all(phase).wait_send()
    for phase, (ref, rows) in enumerate(((right, most), (right, least), (left, full))):
        for d in range(2):
            part = ref.at[s, rows]
            s_copy(phase, part, part, s, mate(d)).wait_send()
        passing_on(phase, ref, rows).wait_send()
    for which in range(2):
        loop(S - 1, lambda d, w=which: give(w, d).wait_send())
    early[4]()
    middle[4]()
    late[4]()


def hand_over(a, b, c, a_out, b_out, c_out, a_v, b_v, c_v, sems):
    held = (a_v, b_v, c_v)
    ins = [pltpu.make_async_copy(x, v, sems.at[k]) for k, (x, v) in enumerate(zip((a, b, c), held))]
    outs = [
        pltpu.make_async_copy(v, x, sems.at[3 + k])
        for k, (x, v) in enumerate(zip((a_out, b_out, c_out), held))
    ]
    for copy in ins:
        copy.start()
    for k in range(3):
        ins[k].wait()
        outs[k].start()
    for copy in outs:
        copy.wait()


def on_device(pair, pair_mask, weights, cotangent):
    pixels = pair.shape[0] * pair.shape[1]
    mask = pair_mask.astype(F32).reshape(3, 16, 3, 8).transpose(0, 2, 1, 3).reshape(BLOCKS, 1, C)
    vmem = pl.BlockSpec(memory_space=pltpu.VMEM)
    anywhere = pl.BlockSpec(memory_space=pl.ANY)

    def sems(*shape):
        return [pltpu.SemaphoreType.DMA(shape)] * 2

    def sum_buffers():
        return [
            *[pltpu.VMEM((W, 8, C), F32)] * 2,
            pltpu.VMEM((8, C), F32),
            pltpu.VMEM((Z, 8, C), F32),
            pltpu.VMEM((8, C), F32),
            pltpu.VMEM((W, 8, C), F32),
        ]

    y_buffers = [pltpu.VMEM((G, len(items), 16, C), BF16) for items in PHASES]
    z_buffers = [pltpu.VMEM((Z, rows, C), BF16) for rows in HELD]
    update, grad_pair, grad_weights = pl.pallas_call(
        kernel,
        out_shape=(
            jax.ShapeDtypeStruct((pixels, C), BF16),
            jax.ShapeDtypeStruct((pixels, C), F32),
            jax.ShapeDtypeStruct((6, C, C), F32),
        ),
        in_specs=[anywhere] * 3 + [vmem] * 2,
        out_specs=(anywhere, anywhere, vmem),
        scratch_shapes=[
            pltpu.VMEM((pixels, C), BF16),
            pltpu.VMEM((pixels, C), BF16),
            pltpu.VMEM((S, ROWS, WIDE), BF16),
            pltpu.VMEM((pixels, C), BF16),
            pltpu.VMEM((pixels, C), F32),
            pltpu.VMEM((6 * C, C), BF16),
            pltpu.VMEM((C, 5 * C), BF16),
            pltpu.VMEM((BLOCKS, 5 * C, C), F32),
            pltpu.VMEM((BLOCKS, C, C), F32),
            pltpu.VMEM((BLOCKS, C, C), BF16),
            pltpu.VMEM((BLOCKS, 1, C), F32),
            pltpu.VMEM((BLOCKS, 5 * C, C), BF16),
            pltpu.VMEM((2, BLOCKS, C, C), BF16),
            pltpu.VMEM((Z * max(HELD), C), F32),
            pltpu.VMEM((12 * C, C), F32),
            pltpu.VMEM((S, ROWS, WIDE), BF16),
            pltpu.VMEM((S, ROWS, WIDE), BF16),
            pltpu.VMEM((WIDE, WIDE), BF16),
            pltpu.VMEM((ROWS, WIDE), BF16),
            pltpu.VMEM((8, S * ROWS, C), F32),
            pltpu.VMEM((S, ROWS, 256), BF16),
            *[pltpu.VMEM((S, ROWS, C), BF16)] * 4,
            pltpu.VMEM((C, 6 * C), F32),
            pltpu.VMEM((BLOCKS, C, C), F32),
            pltpu.VMEM((BLOCKS, C, C), F32),
            *y_buffers,
            *y_buffers,
            *z_buffers,
            *z_buffers,
            *[pltpu.VMEM((Z * rows, C), F32) for rows in HELD],
            *[buffer for _ in range(3) for buffer in sum_buffers()],
            *sems(len(PHASES)),
            *sems(len(PHASES)),
            *sems(5, S),
            *[pltpu.SemaphoreType.DMA((3, 2))] * 3,
            pltpu.SemaphoreType.DMA((6,)),
        ],
        compiler_params=pltpu.CompilerParams(
            collective_id=0, has_side_effects=True, vmem_limit_bytes=56 * 1024 * 1024
        ),
    )(
        pair.reshape(pixels, C),
        cotangent.reshape(pixels, C),
        jnp.asarray(column_order()),
        mask,
        weights,
    )
    results = (update, grad_pair, grad_weights)
    update, grad_pair, grad_weights = pl.pallas_call(
        hand_over,
        out_shape=tuple(jax.ShapeDtypeStruct(a.shape, a.dtype) for a in results),
        in_specs=[anywhere] * 3,
        out_specs=(anywhere,) * 3,
        scratch_shapes=[
            *[pltpu.VMEM(a.shape, a.dtype) for a in results],
            pltpu.SemaphoreType.DMA((6,)),
        ],
    )(*results)
    return update.reshape(pair.shape), grad_pair.reshape(pair.shape), grad_weights


def solution(mesh):
    placed = (P("row", "col", None), P("row", "col"), P(), P("row", "col", None))
    return jax.shard_map(
        on_device,
        mesh=mesh,
        in_specs=placed,
        out_specs=(P("row", "col", None), P("row", "col", None), P()),
        check_vma=False,
    )
```
